32 devices in a mesh: prow: 4 (over y, x), pcol: 8 (over z, core).
Axes of the slice: x: 2, y: 2, z: 4, core: 2. Of those that a mesh axis runs over, the one named last changes fastest.
Arguments:
- inverse_top: bfloat16 [64, 64, 128, 128], P('prow', 'pcol'), may hold values from -6 to 6
- rows_one: int32 [8, 32], replicated, may hold values from 0 to 63, as said below
- panel_one: bfloat16 [8, 32, 128, 128], P('pcol', 'prow'), may hold values from -0.09375 to 0.09375
- base_one: float32 [8, 128, 128], P('pcol'), may hold values from -6 to 6
- parent_two: int32 [8], replicated, may hold values from 0 to 7
- order_two: int32 [8, 32], replicated, may hold values from 0 to 31, as said below
- panel_two: bfloat16 [8, 32, 128, 128], P('pcol', 'prow'), may hold values from -0.09375 to 0.09375
- link_two: bfloat16 [8, 128, 128], P('pcol'), may hold values from -0.5 to 0.5
- base_two: float32 [8, 128, 128], P('pcol'), may hold values from -6 to 6
Outputs:
- column_one: bfloat16 [8, 32, 128, 128], P('pcol', 'prow')
- diagonal_one: bfloat16 [8, 128, 128], P('pcol')
- column_two: bfloat16 [8, 32, 128, 128], P('pcol', 'prow')
- upper_two: bfloat16 [8, 128, 128], P('pcol')
- diagonal_two: bfloat16 [8, 128, 128], P('pcol')
The draws below stay inside these ranges and needn't reach their ends.
Inputs may be any that keep to these rules, and one draw needn't show every extreme that they name: For every supernode k and process row p, rows_one[k, p * 8] to rows_one[k, p * 8 + 7] are 8 distinct ancestors between p * 16 and p * 16 + 15. In every draw some process column c holds 8 ancestors (ancestor // 8 == c) of every level-one supernode. Each block order_two[k, p * 8] to order_two[k, p * 8 + 7] is a permutation of p * 8 to p * 8 + 7.
All inputs are finite; a program needn't handle non-finite values.
Results may differ from the reference program's by a relative error of at most 0.024.
Values may be sent and summed in bfloat16 or wider, within the bound.
No kernel may reach another device: no remote copies, remote signals or barrier semaphores. Data moves between devices by JAX's collectives and lax.ppermute only.
A program may use at most 192 MiB of HBM per device.

```python
import math
from functools import partial
import jax
import jax.numpy as jnp
import numpy as np
from jax import lax

TILE = 128
AP = 16
MP = 8
PCOLS = 8
NA = 64
AQ = 8
M = 32
NS1 = 8
NS2 = 8


def draw_rows_one(key, part):
    groups = M // MP
    split_keys = jax.random.split(jax.random.fold_in(key, 11), NS1 * groups)
    shuffled = jax.vmap(partial(jax.random.permutation, x=AP))(split_keys)
    picked = shuffled[:, :MP].reshape(NS1, groups, MP)
    full_keys = jax.random.split(jax.random.fold_in(key, 12), NS1)
    filled = jax.vmap(partial(jax.random.permutation, x=AQ))(full_keys)[:, :MP]
    chosen = jax.random.randint(jax.random.fold_in(key, 13), (2,), 0, 1 << 20)
    full_row = chosen[0] % groups
    full_class = chosen[1] % (AP // AQ)
    offsets = (jnp.arange(groups, dtype=jnp.int32) * AP)[None, :, None]
    drawn = offsets + picked
    special = (full_row * AP + full_class * AQ + filled)[:, None, :]
    is_full = (jnp.arange(groups, dtype=jnp.int32) == full_row)[None, :, None]
    return jnp.where(is_full, special, drawn).reshape(NS1, M).astype(jnp.int32)


def draw_order_two(key, part):
    groups = M // MP
    key_list = jax.random.split(jax.random.fold_in(key, 21), NS2 * groups)
    shuffled = jax.vmap(partial(jax.random.permutation, x=MP))(key_list).reshape(NS2, groups, MP)
    offsets = (jnp.arange(groups, dtype=jnp.int32) * MP)[None, :, None]
    return (shuffled + offsets).reshape(NS2, M).astype(jnp.int32)


def with_ends(array, stream_key, smallest, top_value):
    index_at = [jax.random.randint(jax.random.fold_in(stream_key, axis), (), 0, length) for axis, length in enumerate(array.shape)]
    longest = array.shape.index(max(array.shape))
    next_to = index_at[:longest] + [(index_at[longest] + 1) % array.shape[longest]] + index_at[longest + 1:]
    return array.at[tuple(index_at)].set(smallest).at[tuple(next_to)].set(top_value)


def block_levels(stream_key, dims, pieces, smallest, top_value):
    def one(dim, parts):
        heights = jax.random.uniform(jax.random.fold_in(jax.random.fold_in(stream_key, 6), dim), (parts,), jnp.float32, smallest / len(pieces), top_value / len(pieces))
        return jnp.repeat(jnp.exp(heights), dims[dim] // parts).reshape((-1,) + (1,) * (len(dims) - dim - 1))

    gain = one(*pieces[0])
    for cut in pieces[1:]:
        gain = gain * one(*cut)
    return gain


def rank_bounds(amount, slope):
    portions = [(1 << 20) // math.isqrt(rank ** slope) + 1 for rank in range(1, amount + 1)]
    scale = 1 + sum(portions) // (1 << 30)
    return np.cumsum(np.array([max(1, weight // scale) for weight in portions]))


def ranked_ids(key, shape, amount, skew):
    table = rank_bounds(amount, skew)
    ticket = jax.random.randint(jax.random.fold_in(key, 1), shape, 0, int(table[amount - 1]))
    standing = jnp.searchsorted(jnp.asarray(table, jnp.int32), ticket, side="right")
    return jax.random.permutation(jax.random.fold_in(key, 2), amount)[standing].astype(jnp.int32)


def scatter_about(own_key, dims, width, limit, cuts=(), held_as=jnp.bfloat16):
    loudness = block_levels(own_key, dims, cuts, -0.22, 0.18) if cuts else 1.0
    entries = jax.random.normal(own_key, dims, jnp.float32) * width * loudness
    return jnp.minimum(jnp.maximum(entries, -limit), limit).astype(held_as)


def setup_inputs(seed: int = 0) -> dict:
    streams_of = jax.random.split(jax.random.key(seed), 10)
    return {
        "inverse_top": scatter_about(streams_of[0], (NA, NA, TILE, TILE), 1.0, 6.0, ((0, 4), (1, 8))),
        "rows_one": draw_rows_one(jax.random.fold_in(streams_of[9], 71), 0),
        "panel_one": scatter_about(streams_of[2], (NS1, M, TILE, TILE), (M * TILE) ** -0.5, 0.09375, ((0, 8), (1, 4))),
        "base_one": scatter_about(streams_of[3], (NS1, TILE, TILE), 1.0, 6.0, ((0, 8),), jnp.float32),
        "parent_two": with_ends(ranked_ids(streams_of[4], (NS2,), NS1, 2), jax.random.fold_in(streams_of[4], 3), 0, NS1 - 1).astype(jnp.int32),
        "order_two": draw_order_two(jax.random.fold_in(streams_of[9], 71), 0),
        "panel_two": scatter_about(streams_of[6], (NS2, M, TILE, TILE), (M * TILE) ** -0.5, 0.09375, ((0, 8), (1, 4))),
        "link_two": scatter_about(streams_of[7], (NS2, TILE, TILE), TILE ** -0.5, 0.5, ((0, 8),)),
        "base_two": scatter_about(streams_of[8], (NS2, TILE, TILE), 1.0, 6.0, ((0, 8),), jnp.float32),
    }


def level_columns(inverse_top, ancestor_rows, panel_tiles):
    classes = jnp.arange(PCOLS, dtype=jnp.int32)

    def one_node(operands):
        ancestors, panels = operands
        submatrix = inverse_top[ancestors[:, None], ancestors[None, :]].astype(jnp.float32)
        products = jnp.einsum("mnij,njk->mnik", submatrix, panels.astype(jnp.float32))
        member = (ancestors[None, :] // AQ == classes[:, None]).astype(jnp.float32)
        partial_value = jnp.einsum("qn,mnik->qmik", member, products).astype(jnp.bfloat16)
        partial_value = lax.optimization_barrier(partial_value).astype(jnp.float32)
        return -jnp.sum(partial_value, axis=0)

    return lax.map(one_node, (ancestor_rows, panel_tiles))


def reference(inverse_top, rows_one, panel_one, base_one, parent_two, order_two, panel_two, link_two, base_two):
    column_one = level_columns(inverse_top, rows_one, panel_one).astype(jnp.bfloat16)
    diag_sum = jnp.einsum("kmij,kmil->kjl", panel_one.astype(jnp.float32), column_one.astype(jnp.float32))
    diagonal_one = (base_one - diag_sum).astype(jnp.bfloat16)
    rows_two = jnp.take_along_axis(rows_one[parent_two], order_two, axis=1)
    terms_two = level_columns(inverse_top, rows_two, panel_two)
    near_two = column_one[parent_two[:, None], order_two]
    carried = jnp.einsum("kmij,kjl->kmil", near_two.astype(jnp.float32), link_two.astype(jnp.float32))
    column_two = (terms_two - carried).astype(jnp.bfloat16)
    parent_term = jnp.einsum("kij,kjl->kil", diagonal_one[parent_two].astype(jnp.float32), link_two.astype(jnp.float32))
    upper_sum = jnp.einsum("kmij,kmil->kjl", near_two.astype(jnp.float32), panel_two.astype(jnp.float32))
    upper_two = (-(parent_term + upper_sum)).astype(jnp.bfloat16)
    link_term = jnp.einsum("kij,kil->kjl", link_two.astype(jnp.float32), upper_two.astype(jnp.float32))
    lower_sum = jnp.einsum("kmij,kmil->kjl", panel_two.astype(jnp.float32), column_two.astype(jnp.float32))
    diagonal_two = (base_two - link_term - lower_sum).astype(jnp.bfloat16)
    return (column_one, diagonal_one, column_two, upper_two, diagonal_two)
```

```python
import functools

import jax
import jax.numpy as jnp
from jax import lax
from jax.experimental import pallas as pl
from jax.experimental.pallas import tpu as pltpu
from jax.sharding import Mesh, PartitionSpec as P

ROW, CHIP, CORE = "prow", "pchip", "pcore"
F32 = jnp.float32
BF16 = jnp.bfloat16


def exchange(x, axis, step):
    size = lax.axis_size(axis)
    return lax.ppermute(x, axis, [(i, i ^ step) for i in range(size)])


def spread(x, axis):
    return [x] + [exchange(x, axis, s) for s in range(1, lax.axis_size(axis))]


def load_inverse(own, sibling, inverse, sems):
    copies = [
        pltpu.make_async_copy(own, inverse.at[0], sems.at[0]),
        pltpu.make_async_copy(sibling, inverse.at[1], sems.at[1]),
    ]
    for copy in copies:
        copy.start()
    return copies


def load_panels(pieces, panels, sems, at):
    group = pieces[0].shape[1]
    copies = []
    for s, piece in enumerate(pieces):
        place = pl.ds(pl.multiple_of((at ^ s) * group, group), group)
        copies.append(pltpu.make_async_copy(piece, panels.at[:, place], sems.at[2 + s]))
        copies[-1].start()
    return copies


def block_row(inverse, row, cols, core, width):
    tiles = [inverse[(col // width) ^ core, row, col % width] for col in cols]
    return jnp.concatenate(tiles, axis=1)


def level_one_kernel(
    nodes, group_rows, rows_one, own, sibling, *refs
):
    height, width = own.shape[0], own.shape[1]
    here, chip, core = lax.axis_index(ROW), lax.axis_index(CHIP), lax.axis_index(CORE)
    pieces, refs = refs[:group_rows], refs[group_rows:]
    whole, sends, (inverse, panels, sems) = refs[0], refs[1:nodes], refs[nodes:]
    per_row, tile = panels.shape[1], panels.shape[2]
    copies = load_inverse(own, sibling, inverse, sems) + load_panels(pieces, panels, sems, here)
    for copy in copies:
        copy.wait()
    for t in range(nodes):
        at = chip ^ t
        node = 2 * at + core
        cols = [rows_one[node, chip * per_row + n] - chip * 2 * width for n in range(per_row)]
        stacked = panels[at].reshape(per_row * tile, tile)
        for m in range(per_row):
            row = rows_one[node, here * per_row + m] - here * height
            part = jnp.dot(
                block_row(inverse, row, cols, core, width), stacked, preferred_element_type=F32
            ).astype(BF16)
            whole[t, m] = part
            if t:
                sends[t - 1][m] = part


def level_two_kernel(
    nodes, group_rows, rows_one, parent_two, order_two, own, sibling, ours, theirs, *refs
):
    height, width = own.shape[0], own.shape[1]
    here, chip, core = lax.axis_index(ROW), lax.axis_index(CHIP), lax.axis_index(CORE)
    pieces, refs = refs[:group_rows], refs[group_rows:]
    factors, refs = refs[:nodes], refs[nodes:]
    columns, smalls, refs = refs[:nodes], refs[nodes : 2 * nodes], refs[2 * nodes :]
    inverse, panels, near, sems = refs
    per_row, tile = panels.shape[1], panels.shape[2]
    copies = load_inverse(own, sibling, inverse, sems) + load_panels(pieces, panels, sems, here)
    for copy in copies:
        copy.wait()
    for t in range(nodes):
        at = chip ^ t
        node = 2 * at + core
        parent = parent_two[node]
        is_ours = parent % 2 == core
        parent_at = (parent // 2) ^ chip
        cols = [
            rows_one[parent, order_two[node, chip * per_row + n]] - chip * 2 * width
            for n in range(per_row)
        ]
        stacked = panels[at].reshape(per_row * tile, tile)
        link = factors[t][per_row]
        for m in range(per_row):
            place = order_two[node, here * per_row + m]
            row = rows_one[parent, place] - here * height
            local = place - here * per_row
            near_tile = jnp.where(is_ours, ours[parent_at, local], theirs[parent_at, local])
            near[m] = near_tile
            part = jnp.dot(
                block_row(inverse, row, cols, core, width), stacked, preferred_element_type=F32
            ) - jnp.dot(near_tile, link, preferred_element_type=F32)
            columns[t][m] = part.astype(BF16)
        factor = factors[t][:per_row].reshape(per_row * tile, tile)
        contract = (((0,), (0,)), ((), ()))
        smalls[t][0] = lax.dot_general(
            near[...].reshape(per_row * tile, tile), factor, contract, preferred_element_type=F32
        ).astype(BF16)
        smalls[t][1] = lax.dot_general(
            factor,
            columns[t][...].reshape(per_row * tile, tile),
            contract,
            preferred_element_type=F32,
        ).astype(BF16)


SMEM = pl.BlockSpec(memory_space=pltpu.SMEM)
VMEM = pl.BlockSpec(memory_space=pltpu.VMEM)
ANY = pl.BlockSpec(memory_space=pl.ANY)


def level_one(rows_one, own, sibling, pieces):
    nodes, group, tile = pieces[0].shape[0], pieces[0].shape[1], pieces[0].shape[2]
    count = len(pieces)
    per_row = group * count
    flops = 2 * nodes * per_row * per_row * tile**3
    return pl.pallas_call(
        functools.partial(level_one_kernel, nodes, count),
        out_shape=[jax.ShapeDtypeStruct((nodes, per_row, tile, tile), BF16)]
        + [jax.ShapeDtypeStruct((per_row, tile, tile), BF16)] * (nodes - 1),
        in_specs=[SMEM, ANY, ANY] + [ANY] * count,
        out_specs=[VMEM] * nodes,
        scratch_shapes=[
            pltpu.VMEM((2,) + own.shape, BF16),
            pltpu.VMEM((nodes, per_row, tile, tile), BF16),
            pltpu.SemaphoreType.DMA((2 + count,)),
        ],
        compiler_params=pltpu.CompilerParams(vmem_limit_bytes=48 << 20),
        cost_estimate=pl.CostEstimate(flops=flops, bytes_accessed=12 << 20, transcendentals=0),
        name="level_one",
    )(rows_one, own, sibling, *pieces)


def level_two(rows_one, parent_two, order_two, own, sibling, ours, theirs, pieces, factors):
    nodes, group, tile = pieces[0].shape[0], pieces[0].shape[1], pieces[0].shape[2]
    count = len(pieces)
    per_row = group * count
    flops = 2 * nodes * per_row * (per_row + 3) * tile**3
    return pl.pallas_call(
        functools.partial(level_two_kernel, nodes, count),
        out_shape=[jax.ShapeDtypeStruct((per_row, tile, tile), BF16)] * nodes
        + [jax.ShapeDtypeStruct((2, tile, tile), BF16)] * nodes,
        in_specs=[SMEM] * 3 + [ANY, ANY, VMEM, VMEM] + [ANY] * count + [VMEM] * nodes,
        out_specs=[VMEM] * (2 * nodes),
        scratch_shapes=[
            pltpu.VMEM((2,) + own.shape, BF16),
            pltpu.VMEM((nodes, per_row, tile, tile), BF16),
            pltpu.VMEM((per_row, tile, tile), BF16),
            pltpu.SemaphoreType.DMA((2 + count,)),
        ],
        compiler_params=pltpu.CompilerParams(vmem_limit_bytes=56 << 20),
        cost_estimate=pl.CostEstimate(flops=flops, bytes_accessed=16 << 20, transcendentals=0),
        name="level_two",
    )(rows_one, parent_two, order_two, own, sibling, ours, theirs, *pieces, *factors)


def distribute(panel):
    rows = lax.axis_size(ROW)
    quarters = panel.reshape((rows, panel.shape[0] // rows) + panel.shape[1:])
    quarters = lax.all_to_all(quarters, ROW, 0, 0, tiled=True)
    quarters = lax.all_to_all(quarters, CHIP, 0, 0, tiled=True)
    return spread(quarters, ROW)


def total(parts):
    return functools.reduce(jnp.add, [part.astype(F32) for part in parts])


def local(
    inverse_top, rows_one, panel_one, base_one, parent_two, order_two, panel_two, link_two, base_two
):
    chip, core = lax.axis_index(CHIP), lax.axis_index(CORE)
    sibling = exchange(inverse_top, CORE, 1)
    pieces_one = distribute(panel_one[0])
    pieces_two = distribute(panel_two[0])
    factors = spread(jnp.concatenate([panel_two[0], link_two], axis=0), CHIP)
    ours, *sends = level_one(rows_one, inverse_top, sibling, pieces_one)
    theirs = exchange(ours, CORE, 1)
    parts_one = [ours[0]] + [exchange(send, CHIP, t + 1) for t, send in enumerate(sends)]
    outs = level_two(
        rows_one, parent_two, order_two, inverse_top, sibling, ours, theirs, pieces_two, factors
    )
    nodes = len(outs) // 2
    parts_two = [outs[0]] + [exchange(outs[t], CHIP, t) for t in range(1, nodes)]
    parts_small = [outs[nodes]] + [exchange(outs[nodes + t], CHIP, t) for t in range(1, nodes)]
    column_one = (-total(parts_one)).astype(BF16)
    column_two = (-total(parts_two)).astype(BF16)
    sums = total(spread(total(parts_small).astype(BF16), ROW))
    part = jnp.einsum("mij,mil->jl", panel_one[0], column_one, preferred_element_type=F32)
    diagonal_one = (base_one[0] - total(spread(part.astype(BF16), ROW))).astype(BF16)
    pair = jnp.stack([diagonal_one, exchange(diagonal_one, CORE, 1)])
    diagonals = jnp.stack(spread(pair, CHIP))
    parent = parent_two[2 * chip + core]
    near_diagonal = diagonals[(parent // 2) ^ chip, (parent % 2) ^ core]
    link = link_two[0]
    upper = (sums[0] - jnp.dot(near_diagonal, link, preferred_element_type=F32)).astype(BF16)
    link_term = jnp.einsum("ij,il->jl", link, upper, preferred_element_type=F32)
    diagonal_two = (base_two[0] - link_term + sums[1]).astype(BF16)
    return (
        column_one[None],
        diagonal_one[None],
        column_two[None],
        upper[None],
        diagonal_two[None],
    )


def solution(mesh):
    rows, columns = mesh.devices.shape
    fine = Mesh(mesh.devices.reshape(rows, columns // 2, 2), (ROW, CHIP, CORE))
    col = (CHIP, CORE)
    return jax.shard_map(
        local,
        mesh=fine,
        in_specs=(
            P(ROW, col, None, None),
            P(),
            P(col, ROW, None, None),
            P(col, None, None),
            P(),
            P(),
            P(col, ROW, None, None),
            P(col, None, None),
            P(col, None, None),
        ),
        out_specs=(
            P(col, ROW, None, None),
            P(col, None, None),
            P(col, ROW, None, None),
            P(col, None, None),
            P(col, None, None),
        ),
        check_vma=False,
    )
```

```python
import functools

import jax
import jax.numpy as jnp
from jax import lax
from jax.experimental import pallas as pl
from jax.experimental.pallas import tpu as pltpu
from jax.sharding import Mesh, PartitionSpec as P

ROW, CHIP, CORE = "prow", "pchip", "pcore"
F32 = jnp.float32
BF16 = jnp.bfloat16


def exchange(x, axis, step):
    size = lax.axis_size(axis)
    return lax.ppermute(x, axis, [(i, i ^ step) for i in range(size)])


def spread(x, axis):
    return [x] + [exchange(x, axis, s) for s in range(1, lax.axis_size(axis))]


def load_inverse(own, sibling, inverse, sems):
    copies = [
        pltpu.make_async_copy(own, inverse.at[0], sems.at[0]),
        pltpu.make_async_copy(sibling, inverse.at[1], sems.at[1]),
    ]
    for copy in copies:
        copy.start()
    return copies


def load_panels(pieces, panels, sems, at):
    group = pieces[0].shape[1]
    copies = []
    for s, piece in enumerate(pieces):
        place = pl.ds(pl.multiple_of((at ^ s) * group, group), group)
        copies.append(pltpu.make_async_copy(piece, panels.at[:, place], sems.at[2 + s]))
        copies[-1].start()
    return copies


def block_row(inverse, row, cols, core, width):
    tiles = [inverse[(col // width) ^ core, row, col % width] for col in cols]
    return jnp.concatenate(tiles, axis=1)


def level_one_kernel(
    nodes, group_rows, rows_one, own, sibling, *refs
):
    height, width = own.shape[0], own.shape[1]
    here, chip, core = lax.axis_index(ROW), lax.axis_index(CHIP), lax.axis_index(CORE)
    pieces, refs = refs[:group_rows], refs[group_rows:]
    whole, inverse, panels, sems = refs
    per_row, tile = panels.shape[1], panels.shape[2]
    copies = load_inverse(own, sibling, inverse, sems) + load_panels(pieces, panels, sems, here)
    for copy in copies:
        copy.wait()
    for at in range(nodes):
        node = 2 * at + core
        cols = [rows_one[node, chip * per_row + n] - chip * 2 * width for n in range(per_row)]
        stacked = panels[at].reshape(per_row * tile, tile)
        for m in range(per_row):
            row = rows_one[node, here * per_row + m] - here * height
            whole[at, m] = jnp.dot(
                block_row(inverse, row, cols, core, width), stacked, preferred_element_type=F32
            ).astype(BF16)


def level_two_kernel(
    nodes, group_rows, choices, rows_one, parent_two, order_two, own, sibling, ours, theirs, *refs
):
    height, width = own.shape[0], own.shape[1]
    here, chip, core = lax.axis_index(ROW), lax.axis_index(CHIP), lax.axis_index(CORE)
    pieces, refs = refs[:group_rows], refs[group_rows:]
    inputs, refs = refs[: sum(choices)], refs[sum(choices) :]
    columns, smalls, refs = refs[:nodes], refs[nodes : 2 * nodes], refs[2 * nodes :]
    inverse, panels, near, sems = refs
    is_end = jnp.logical_or(chip == 0, chip == nodes - 1)
    factors = []
    for count in choices:
        factors.append(inputs[:count])
        inputs = inputs[count:]
    per_row, tile = panels.shape[1], panels.shape[2]
    copies = load_inverse(own, sibling, inverse, sems) + load_panels(pieces, panels, sems, here)
    for copy in copies:
        copy.wait()
    for t in range(nodes):
        at = chip ^ t
        node = 2 * at + core
        parent = parent_two[node]
        is_ours = parent % 2 == core
        parent_at = parent // 2
        cols = [
            rows_one[parent, order_two[node, chip * per_row + n]] - chip * 2 * width
            for n in range(per_row)
        ]
        stacked = panels[at].reshape(per_row * tile, tile)
        factor = factors[t][0][...]
        if len(factors[t]) > 1:
            factor = jnp.where(is_end, factors[t][1][...], factor)
        link = factor[per_row]
        for m in range(per_row):
            place = order_two[node, here * per_row + m]
            row = rows_one[parent, place] - here * height
            local = place - here * per_row
            near_tile = jnp.where(is_ours, ours[parent_at, local], theirs[parent_at, local])
            near[m] = near_tile
            part = jnp.dot(
                block_row(inverse, row, cols, core, width), stacked, preferred_element_type=F32
            ) - jnp.dot(near_tile, link, preferred_element_type=F32)
            columns[t][m] = part.astype(BF16)
        factor = factor[:per_row].reshape(per_row * tile, tile)
        contract = (((0,), (0,)), ((), ()))
        smalls[t][0] = lax.dot_general(
            near[...].reshape(per_row * tile, tile), factor, contract, preferred_element_type=F32
        ).astype(BF16)
        smalls[t][1] = lax.dot_general(
            factor,
            columns[t][...].reshape(per_row * tile, tile),
            contract,
            preferred_element_type=F32,
        ).astype(BF16)


SMEM = pl.BlockSpec(memory_space=pltpu.SMEM)
VMEM = pl.BlockSpec(memory_space=pltpu.VMEM)
ANY = pl.BlockSpec(memory_space=pl.ANY)


def level_one(rows_one, own, sibling, pieces):
    nodes, group, tile = pieces[0].shape[0], pieces[0].shape[1], pieces[0].shape[2]
    count = len(pieces)
    per_row = group * count
    flops = 2 * nodes * per_row * per_row * tile**3
    return pl.pallas_call(
        functools.partial(level_one_kernel, nodes, count),
        out_shape=jax.ShapeDtypeStruct((nodes, per_row, tile, tile), BF16),
        in_specs=[SMEM, ANY, ANY] + [ANY] * count,
        out_specs=VMEM,
        scratch_shapes=[
            pltpu.VMEM((2,) + own.shape, BF16),
            pltpu.VMEM((nodes, per_row, tile, tile), BF16),
            pltpu.SemaphoreType.DMA((2 + count,)),
        ],
        compiler_params=pltpu.CompilerParams(vmem_limit_bytes=48 << 20),
        cost_estimate=pl.CostEstimate(flops=flops, bytes_accessed=12 << 20, transcendentals=0),
        name="level_one",
    )(rows_one, own, sibling, *pieces)


def level_two(rows_one, parent_two, order_two, own, sibling, ours, theirs, pieces, factors):
    nodes, group, tile = pieces[0].shape[0], pieces[0].shape[1], pieces[0].shape[2]
    count = len(pieces)
    per_row = group * count
    flops = 2 * nodes * per_row * (per_row + 3) * tile**3
    return pl.pallas_call(
        functools.partial(level_two_kernel, nodes, count, [len(f) for f in factors]),
        out_shape=[jax.ShapeDtypeStruct((per_row, tile, tile), BF16)] * nodes
        + [jax.ShapeDtypeStruct((2, tile, tile), BF16)] * nodes,
        in_specs=[SMEM] * 3 + [ANY, ANY, VMEM, VMEM] + [ANY] * count + [VMEM] * sum(len(f) for f in factors),
        out_specs=[VMEM] * (2 * nodes),
        scratch_shapes=[
            pltpu.VMEM((2,) + own.shape, BF16),
            pltpu.VMEM((nodes, per_row, tile, tile), BF16),
            pltpu.VMEM((per_row, tile, tile), BF16),
            pltpu.SemaphoreType.DMA((2 + count,)),
        ],
        compiler_params=pltpu.CompilerParams(vmem_limit_bytes=56 << 20),
        cost_estimate=pl.CostEstimate(flops=flops, bytes_accessed=16 << 20, transcendentals=0),
        name="level_two",
    )(rows_one, parent_two, order_two, own, sibling, ours, theirs, *pieces, *sum(factors, []))


def after(x, *others):
    return lax.optimization_barrier((x,) + others)[0]


def halves(panel, axis):
    rows = lax.axis_size(axis)
    return panel.reshape((rows, panel.shape[0] // rows) + panel.shape[1:])


def send(x, axis, pairs):
    return lax.ppermute(x, axis, pairs)


def swap(blocks, axis):
    return lax.all_to_all(blocks, axis, 0, 0, tiled=True)


def total(parts):
    return functools.reduce(jnp.add, [part.astype(F32) for part in parts])


def local(
    inverse_top, rows_one, panel_one, base_one, parent_two, order_two, panel_two, link_two, base_two
):
    chip, core = lax.axis_index(CHIP), lax.axis_index(CORE)
    nodes = lax.axis_size(CHIP)
    line = nodes == 4
    payload = jnp.concatenate([panel_two[0], link_two], axis=0)
    near = exchange(payload, CHIP, 1)
    if line:
        inner = send(payload, CHIP, [(1, 2), (2, 1)])
    else:
        inner = [exchange(payload, CHIP, t) for t in range(2, nodes)]
    sibling = exchange(inverse_top, CORE, 1)
    both = jnp.concatenate([halves(panel_one[0], ROW), halves(panel_two[0], ROW)], axis=1)
    quarters = swap(both, ROW)
    quarters, near, inner = lax.optimization_barrier((quarters, near, inner))
    group = quarters.shape[1] // 2
    blocks_one = swap(quarters[:, :group], CHIP)
    pieces_one = spread(blocks_one, ROW)
    quarters_two, near_late, inner_late, blocks_one = lax.optimization_barrier(
        (quarters[:, group:], near, inner, blocks_one)
    )
    blocks_two = swap(quarters_two, CHIP)
    over = out_one = ()
    if line:
        over = send(near_late, CHIP, [(1, 2), (2, 1)])
        out_one = send(inner_late, CHIP, [(1, 0), (2, 3)])
    pieces_one = lax.optimization_barrier(pieces_one)
    pieces_one, blocks_two, over, out_one = lax.optimization_barrier(
        (pieces_one, blocks_two, over, out_one)
    )
    out_two = send(over, CHIP, [(1, 0), (2, 3)]) if line else ()
    pieces_two = spread(blocks_two, ROW)
    ours = level_one(rows_one, inverse_top, sibling, pieces_one)
    ours, out_two, pieces_two = lax.optimization_barrier((ours, out_two, pieces_two))
    ours_too = ours
    theirs = exchange(ours_too, CORE, 1)
    parts_one = swap(ours, CHIP)
    if line:
        factors = [[payload], [near], [over, out_one], [inner, out_two]]
    else:
        factors = [[f] for f in [payload, near, *inner]]
    outs = level_two(
        rows_one, parent_two, order_two, inverse_top, sibling, ours, theirs, pieces_two, factors
    )
    columns, smalls = outs[:nodes], outs[nodes:]
    parts_small = [smalls[0]] + [exchange(smalls[t], CHIP, t) for t in range(1, nodes)]
    columns, parts_small = lax.optimization_barrier((columns, parts_small))
    column_one = (-jnp.sum(parts_one.astype(F32), axis=0)).astype(BF16)
    part = jnp.einsum("mij,mil->jl", panel_one[0], column_one, preferred_element_type=F32)
    base = jnp.where(lax.axis_index(ROW) == 0, base_one[0], 0)
    share = (base - part).astype(BF16)
    first = [exchange(columns[t], CHIP, t) for t in range(nodes // 2 + 1, nodes)]
    pair = jnp.stack([share, exchange(share, CORE, 1)])
    last, pair = lax.optimization_barrier((columns[1 : nodes // 2 + 1], pair))
    shares = spread(pair, CHIP)
    shares, first = lax.optimization_barrier((shares, first))
    shares = jnp.stack(shares)
    last = [exchange(last[t - 1], CHIP, t) for t in range(1, nodes // 2 + 1)]
    parent = parent_two[2 * chip + core]
    parent_share = shares[(parent // 2) ^ chip, (parent % 2) ^ core]
    small = jnp.concatenate(
        [total(parts_small).astype(BF16), share[None], parent_share[None]], axis=0
    )
    sums, last = lax.optimization_barrier((spread(small, ROW), last))
    sums = total(sums)
    column_two = (-total([columns[0], *first, *last])).astype(BF16)
    diagonal_one = sums[2].astype(BF16)
    near_diagonal = sums[3].astype(BF16)
    link = link_two[0]
    upper = (sums[0] - jnp.dot(near_diagonal, link, preferred_element_type=F32)).astype(BF16)
    link_term = jnp.einsum("ij,il->jl", link, upper, preferred_element_type=F32)
    diagonal_two = (base_two[0] - link_term + sums[1]).astype(BF16)
    return (
        column_one[None],
        diagonal_one[None],
        column_two[None],
        upper[None],
        diagonal_two[None],
    )


def solution(mesh):
    rows, columns = mesh.devices.shape
    fine = Mesh(mesh.devices.reshape(rows, columns // 2, 2), (ROW, CHIP, CORE))
    col = (CHIP, CORE)
    return jax.shard_map(
        local,
        mesh=fine,
        in_specs=(
            P(ROW, col, None, None),
            P(),
            P(col, ROW, None, None),
            P(col, None, None),
            P(),
            P(),
            P(col, ROW, None, None),
            P(col, None, None),
            P(col, None, None),
        ),
        out_specs=(
            P(col, ROW, None, None),
            P(col, None, None),
            P(col, ROW, None, None),
            P(col, None, None),
            P(col, None, None),
        ),
        check_vma=False,
    )
```

```python
import functools

import jax
import jax.numpy as jnp
from jax import lax
from jax.experimental import pallas as pl
from jax.experimental.pallas import tpu as pltpu
from jax.sharding import Mesh, PartitionSpec as P

ROW, CHIP, CORE = "prow", "pchip", "pcore"
F32 = jnp.float32
BF16 = jnp.bfloat16
SMEM = pl.BlockSpec(memory_space=pltpu.SMEM)
VMEM = pl.BlockSpec(memory_space=pltpu.VMEM)
LIMIT = 24 << 20
MOST = 56 << 20


HBM = pl.BlockSpec(memory_space=pltpu.HBM)


def begin(copies):
    for copy in copies:
        copy.start()
    return copies


def finish(copies):
    for copy in copies:
        copy.wait()


def load(own, sibling, inverse, sems):
    core = lax.axis_index(CORE)
    return begin(
        [
            pltpu.make_async_copy(own, inverse.at[core], sems.at[0]),
            pltpu.make_async_copy(sibling, inverse.at[1 - core], sems.at[1]),
        ]
    )


def load_panels(pieces, panels, sems):
    here, group = lax.axis_index(ROW), pieces[0].shape[1]
    copies = []
    for s, piece in enumerate(pieces):
        place = pl.ds(pl.multiple_of((here ^ s) * group, group), group)
        copies.append(pltpu.make_async_copy(piece, panels.at[:, place], sems.at[s]))
    return begin(copies)


def block(inverse, rows, cols):
    width = inverse.shape[2]
    lines = []
    for row in rows:
        tiles = [inverse[col // width, row, col % width] for col in cols]
        lines.append(jnp.concatenate(tiles, axis=1))
    return jnp.concatenate(lines, axis=0)


def level_one_kernel(nodes, count, rows_one, own, sibling, *refs):
    here, chip, core = lax.axis_index(ROW), lax.axis_index(CHIP), lax.axis_index(CORE)
    pieces, refs = refs[:count], refs[count:]
    whole, sends, (inverse, panels, held, sems, out_sems) = refs[0], refs[1:nodes], refs[nodes:]
    per_row, tile = panels.shape[1], panels.shape[2]
    height, width = inverse.shape[1], 2 * inverse.shape[2]
    finish(load(own, sibling, inverse, sems) + load_panels(pieces, panels, sems.at[2:]))
    copies = []
    for t in reversed(range(nodes)):
        at = chip ^ t
        node = 2 * at + core
        rows = [rows_one[node, here * per_row + m] - here * height for m in range(per_row)]
        cols = [rows_one[node, chip * per_row + n] - chip * width for n in range(per_row)]
        panel = panels[at].reshape(per_row * tile, tile)
        part = jnp.dot(block(inverse, rows, cols), panel, preferred_element_type=F32)
        held[t] = part.astype(BF16).reshape(per_row, tile, tile)
        copies += begin([pltpu.make_async_copy(held.at[t], whole.at[at], out_sems.at[t])])
        if t:
            copies += begin(
                [pltpu.make_async_copy(held.at[t], sends[t - 1], out_sems.at[nodes + t])]
            )
    finish(copies)


def level_two_kernel(
    nodes, count, choices, rows_one, parent_two, order_two, own, sibling, ours, theirs, *refs
):
    here, chip, core = lax.axis_index(ROW), lax.axis_index(CHIP), lax.axis_index(CORE)
    pieces, refs = refs[:count], refs[count:]
    inputs, refs = refs[: sum(choices)], refs[sum(choices) :]
    columns, smalls, refs = refs[:nodes], refs[nodes : 2 * nodes], refs[2 * nodes :]
    inverse, panels, blocks, factors, held, sems, in_sems, out_sems = refs
    per_row, tile = panels.shape[1], panels.shape[2]
    height, width = inverse.shape[1], 2 * inverse.shape[2]
    first = begin(
        [
            pltpu.make_async_copy(ours, blocks.at[core], in_sems.at[nodes]),
            pltpu.make_async_copy(theirs, blocks.at[1 - core], in_sems.at[nodes + 1]),
        ]
    )
    is_end = jnp.logical_or(chip == 0, chip == nodes - 1)
    for t in range(nodes):
        mine, inputs = inputs[: choices[t]], inputs[choices[t] :]
        copies = [pltpu.make_async_copy(ref, factors.at[t], in_sems.at[t]) for ref in mine]
        first.append(copies[0])
        if len(copies) == 1:
            copies[0].start()
        else:
            pl.when(is_end)(copies[1].start)
            pl.when(jnp.logical_not(is_end))(copies[0].start)
    second = load(own, sibling, inverse, sems) + load_panels(pieces, panels, sems.at[2:])
    finish(first)
    contract = (((0,), (0,)), ((), ()))
    parts = []
    for t in range(nodes):
        node = 2 * (chip ^ t) + core
        parent = parent_two[node]
        near = [
            blocks[parent % 2, parent // 2, order_two[node, here * per_row + m] - here * per_row]
            for m in range(per_row)
        ]
        near = jnp.concatenate(near, axis=0)
        factor = factors[t, :per_row].reshape(per_row * tile, tile)
        smalls[t][0] = lax.dot_general(near, factor, contract, preferred_element_type=F32).astype(
            BF16
        )
        parts.append(jnp.dot(near, factors[t, per_row], preferred_element_type=F32))
    finish(second)
    copies = []
    for t in reversed(range(nodes)):
        node = 2 * (chip ^ t) + core
        parent = parent_two[node]
        rows = [
            rows_one[parent, order_two[node, here * per_row + m]] - here * height
            for m in range(per_row)
        ]
        cols = [
            rows_one[parent, order_two[node, chip * per_row + n]] - chip * width
            for n in range(per_row)
        ]
        panel = panels[chip ^ t].reshape(per_row * tile, tile)
        part = jnp.dot(block(inverse, rows, cols), panel, preferred_element_type=F32)
        part = (part - parts[t]).astype(BF16)
        held[t] = part.reshape(per_row, tile, tile)
        copies += begin([pltpu.make_async_copy(held.at[t], columns[t], out_sems.at[t])])
        factor = factors[t, :per_row].reshape(per_row * tile, tile)
        smalls[t][1] = lax.dot_general(factor, part, contract, preferred_element_type=F32).astype(
            BF16
        )
    finish(copies)


def column_kernel(parts, panel, column, part):
    column[...] = (-jnp.sum(parts[...].astype(F32), axis=0)).astype(BF16)
    shape = (panel.shape[0] * panel.shape[1], panel.shape[2])
    part[...] = lax.dot_general(
        panel[...].reshape(shape),
        column[...].reshape(shape),
        (((0,), (0,)), ((), ())),
        preferred_element_type=F32,
    ).astype(BF16)


def form_column(parts, panel):
    return pl.pallas_call(
        column_kernel,
        out_shape=[
            jax.ShapeDtypeStruct(panel.shape, BF16),
            jax.ShapeDtypeStruct(panel.shape[1:], BF16),
        ],
        in_specs=[VMEM] * 2,
        out_specs=[VMEM] * 2,
        compiler_params=pltpu.CompilerParams(vmem_limit_bytes=LIMIT),
        name="form_column",
    )(parts, panel)


def choose_kernel(nodes, parent_two, ours, theirs, *outs):
    chip, core = lax.axis_index(CHIP), lax.axis_index(CORE)
    for t in range(nodes):
        parent = parent_two[2 * (chip ^ t) + core]
        outs[t][...] = jnp.where(parent % 2 == core, ours[...], theirs[...])


def choose(nodes, parent_two, ours, theirs):
    return pl.pallas_call(
        functools.partial(choose_kernel, nodes),
        out_shape=[jax.ShapeDtypeStruct(ours.shape, BF16)] * nodes,
        in_specs=[SMEM] + [VMEM] * 2,
        out_specs=[VMEM] * nodes,
        compiler_params=pltpu.CompilerParams(vmem_limit_bytes=LIMIT),
        name="choose",
    )(parent_two, ours, theirs)


def last_kernel(nodes, parent_two, link, base, *refs):
    diagonals, parts, (upper, diagonal_two) = refs[:nodes], refs[nodes:-2], refs[-2:]
    chip, core = lax.axis_index(CHIP), lax.axis_index(CORE)
    step = (parent_two[2 * chip + core] // 2) ^ chip
    near = diagonals[0][...]
    for t in range(1, nodes):
        near = jnp.where(step == t, diagonals[t][...], near)
    sums = total([part[...] for part in parts])
    parent_term = jnp.dot(near, link[...], preferred_element_type=F32)
    upper[...] = (sums[0] - parent_term).astype(BF16)
    term = lax.dot_general(
        link[...], upper[...], (((0,), (0,)), ((), ())), preferred_element_type=F32
    )
    diagonal_two[...] = (base[...] - term + sums[1]).astype(BF16)


def form_last(parent_two, link, base, diagonals, parts):
    return pl.pallas_call(
        functools.partial(last_kernel, len(diagonals)),
        out_shape=[jax.ShapeDtypeStruct(link.shape, BF16)] * 2,
        in_specs=[SMEM] + [VMEM] * (2 + len(diagonals) + len(parts)),
        out_specs=[VMEM] * 2,
        compiler_params=pltpu.CompilerParams(vmem_limit_bytes=LIMIT),
        name="form_last",
    )(parent_two, link, base, *diagonals, *parts)


def level_one(rows_one, own, sibling, pieces):
    nodes, group, tile = pieces[0].shape[0], pieces[0].shape[1], pieces[0].shape[2]
    count = len(pieces)
    per_row = group * count
    flops = 2 * nodes * per_row * per_row * tile**3
    tiles = (per_row, tile, tile)
    return pl.pallas_call(
        functools.partial(level_one_kernel, nodes, count),
        out_shape=[jax.ShapeDtypeStruct((nodes,) + tiles, BF16)]
        + [jax.ShapeDtypeStruct(tiles, BF16)] * (nodes - 1),
        in_specs=[SMEM] + [HBM] * (2 + count),
        out_specs=[HBM] * nodes,
        scratch_shapes=[
            pltpu.VMEM((2,) + own.shape, BF16),
            pltpu.VMEM((nodes,) + tiles, BF16),
            pltpu.VMEM((nodes,) + tiles, BF16),
            pltpu.SemaphoreType.DMA((2 + count,)),
            pltpu.SemaphoreType.DMA((2 * nodes,)),
        ],
        compiler_params=pltpu.CompilerParams(vmem_limit_bytes=MOST),
        cost_estimate=pl.CostEstimate(flops=flops, bytes_accessed=12 << 20, transcendentals=0),
        name="level_one",
    )(rows_one, own, sibling, *pieces)


def level_two(rows_one, parent_two, order_two, own, sibling, ours, theirs, pieces, factors):
    nodes, group, tile = pieces[0].shape[0], pieces[0].shape[1], pieces[0].shape[2]
    count = len(pieces)
    per_row = group * count
    flops = 2 * nodes * per_row * (per_row + 3) * tile**3
    choices = [len(f) for f in factors]
    tiles = (per_row, tile, tile)
    return pl.pallas_call(
        functools.partial(level_two_kernel, nodes, count, choices),
        out_shape=[jax.ShapeDtypeStruct(tiles, BF16)] * nodes
        + [jax.ShapeDtypeStruct((2, tile, tile), BF16)] * nodes,
        in_specs=[SMEM] * 3 + [HBM] * (4 + count + sum(choices)),
        out_specs=[HBM] * nodes + [VMEM] * nodes,
        scratch_shapes=[
            pltpu.VMEM((2,) + own.shape, BF16),
            pltpu.VMEM((nodes,) + tiles, BF16),
            pltpu.VMEM((2, nodes) + tiles, BF16),
            pltpu.VMEM((nodes, per_row + 1, tile, tile), BF16),
            pltpu.VMEM((nodes,) + tiles, BF16),
            pltpu.SemaphoreType.DMA((2 + count,)),
            pltpu.SemaphoreType.DMA((nodes + 2,)),
            pltpu.SemaphoreType.DMA((nodes,)),
        ],
        compiler_params=pltpu.CompilerParams(vmem_limit_bytes=MOST),
        cost_estimate=pl.CostEstimate(flops=flops, bytes_accessed=16 << 20, transcendentals=0),
        name="level_two",
    )(rows_one, parent_two, order_two, own, sibling, ours, theirs, *pieces, *sum(factors, []))


def exchange(x, axis, step):
    size = lax.axis_size(axis)
    return lax.ppermute(x, axis, [(i, i ^ step) for i in range(size)])


def spread(x, axis):
    return [x] + [exchange(x, axis, s) for s in range(1, lax.axis_size(axis))]


def after(x, *others):
    return lax.optimization_barrier((x,) + others)[0]


def together(*arrays):
    return lax.optimization_barrier(arrays)


def halves(panel, axis):
    rows = lax.axis_size(axis)
    return panel.reshape((rows, panel.shape[0] // rows) + panel.shape[1:])


def swap(blocks, axis):
    return lax.all_to_all(blocks, axis, 0, 0, tiled=True)


def total(parts):
    return functools.reduce(jnp.add, [part.astype(F32) for part in parts])


def local(
    inverse_top, rows_one, panel_one, base_one, parent_two, order_two, panel_two, link_two, base_two
):
    chip, core = lax.axis_index(CHIP), lax.axis_index(CORE)
    nodes = lax.axis_size(CHIP)
    line = nodes == 4
    payload = jnp.concatenate([panel_two[0], link_two], axis=0)
    near = exchange(payload, CHIP, 1)
    if line:
        inner = lax.ppermute(payload, CHIP, [(1, 2), (2, 1)])
    else:
        inner = [exchange(payload, CHIP, t) for t in range(2, nodes)]
    sibling = exchange(inverse_top, CORE, 1)
    both = jnp.concatenate([halves(panel_one[0], ROW), halves(panel_two[0], ROW)], axis=1)
    quarters = swap(both, ROW)
    quarters, near, inner = together(quarters, near, inner)
    group = quarters.shape[1] // 2
    blocks_one = swap(quarters[:, :group], CHIP)
    pieces_one = spread(blocks_one, ROW)
    quarters_two, payload_late, near_late, inner_late = together(
        quarters[:, group:], payload, near, inner, blocks_one
    )[:4]
    blocks_two = swap(quarters_two, CHIP)
    over = out_one = out_two = ()
    if line:
        over = lax.ppermute(near_late, CHIP, [(1, 2), (2, 1)])
        out_one = lax.ppermute(inner_late, CHIP, [(1, 0), (2, 3)])
        out_two = lax.ppermute(payload_late, CHIP, [(0, 3), (3, 0)])
    ours, *sends = level_one(rows_one, inverse_top, sibling, pieces_one)
    pieces_two = spread(blocks_two, ROW)
    ours, over, out_one, out_two, pieces_two = together(ours, over, out_one, out_two, pieces_two)
    theirs = exchange(ours, CORE, 1)
    parts_one = swap(ours, CHIP)
    if line:
        factors = [[payload], [near], [over, out_one], [inner, out_two]]
    else:
        factors = [[f] for f in [payload, near, *inner]]
    outs = level_two(
        rows_one, parent_two, order_two, inverse_top, sibling, ours, theirs, pieces_two, factors
    )
    columns, smalls = outs[:nodes], outs[nodes:]
    first = [exchange(columns[t], CHIP, t) for t in range(nodes // 2 + 1, nodes)]
    parts_small = [smalls[0]] + [exchange(smalls[t], CHIP, t) for t in range(1, nodes)]
    *last, token = together(*columns[1 : nodes // 2 + 1], parts_small)
    last = [exchange(column, CHIP, t + 1) for t, column in enumerate(last)]
    column_one, part = form_column(parts_one, panel_one[0])
    diagonal_one = (base_one[0] - total(spread(part, ROW))).astype(BF16)
    chosen = choose(nodes, parent_two, diagonal_one, exchange(diagonal_one, CORE, 1))
    diagonals = [chosen[0]] + [exchange(chosen[t], CHIP, t) for t in range(1, nodes)]
    parts_last = spread(total(parts_small).astype(BF16), ROW)
    upper, diagonal_two = form_last(parent_two, link_two[0], base_two[0], diagonals, parts_last)
    column_two = (-total([columns[0], *first, *last])).astype(BF16)
    return (
        column_one[None],
        diagonal_one[None],
        column_two[None],
        upper[None],
        diagonal_two[None],
    )


def solution(mesh):
    rows, columns = mesh.devices.shape
    fine = Mesh(mesh.devices.reshape(rows, columns // 2, 2), (ROW, CHIP, CORE))
    col = (CHIP, CORE)
    return jax.shard_map(
        local,
        mesh=fine,
        in_specs=(
            P(ROW, col, None, None),
            P(),
            P(col, ROW, None, None),
            P(col, None, None),
            P(),
            P(),
            P(col, ROW, None, None),
            P(col, None, None),
            P(col, None, None),
        ),
        out_specs=(
            P(col, ROW, None, None),
            P(col, None, None),
            P(col, ROW, None, None),
            P(col, None, None),
            P(col, None, None),
        ),
        check_vma=False,
    )
```

```python
import functools

import jax
import jax.numpy as jnp
from jax import lax
from jax.experimental import pallas as pl
from jax.experimental.pallas import tpu as pltpu
from jax.sharding import Mesh, PartitionSpec as P

ROW, CHIP, CORE = "prow", "pchip", "pcore"
F32 = jnp.float32
BF16 = jnp.bfloat16
SMEM = pl.BlockSpec(memory_space=pltpu.SMEM)
VMEM = pl.BlockSpec(memory_space=pltpu.VMEM)
LIMIT = 24 << 20
PARTS = 4


HBM = pl.BlockSpec(memory_space=pltpu.HBM)
ANY = pl.BlockSpec(memory_space=pl.ANY)


def begin(copies):
    for copy in copies:
        copy.start()
    return copies


def finish(copies):
    for copy in copies:
        copy.wait()


def load(own, sibling, inverse, sems):
    core, step = lax.axis_index(CORE), own.shape[0] // PARTS
    copies = []
    for n in range(PARTS):
        rows = pl.ds(n * step, step)
        for k, (ref, at) in enumerate(((own, core), (sibling, 1 - core))):
            copies.append(
                pltpu.make_async_copy(ref.at[rows], inverse.at[at, rows], sems.at[2 * n + k])
            )
    return begin(copies)


def pair_kernel(own, sibling, inverse, sems):
    finish(load(own, sibling, inverse, sems))


def pair(own, sibling):
    return pl.pallas_call(
        pair_kernel,
        out_shape=jax.ShapeDtypeStruct((2,) + own.shape, BF16),
        in_specs=[ANY] * 2,
        out_specs=VMEM,
        scratch_shapes=[pltpu.SemaphoreType.DMA((2 * PARTS,))],
        compiler_params=pltpu.CompilerParams(vmem_limit_bytes=LIMIT),
        name="pair",
    )(own, sibling)


def positions(count, group, here):
    return [(here ^ s) * group + g for s in range(count) for g in range(group)]


def block(inverse, rows, cols):
    width = inverse.shape[2]
    lines = []
    for row in rows:
        tiles = [inverse[col // width, row, col % width] for col in cols]
        lines.append(jnp.concatenate(tiles, axis=1))
    return jnp.concatenate(lines, axis=0)


def level_one_kernel(nodes, count, rows_one, inverse, *refs):
    here, chip, core = lax.axis_index(ROW), lax.axis_index(CHIP), lax.axis_index(CORE)
    pieces, whole = refs[:count], refs[count]
    group, tile = pieces[0].shape[1], pieces[0].shape[2]
    per_row = group * count
    height, width = inverse.shape[1], 2 * inverse.shape[2]
    for at in range(nodes):
        node = 2 * at + core
        rows = [rows_one[node, here * per_row + m] - here * height for m in range(per_row)]
        cols = [
            rows_one[node, chip * per_row + n] - chip * width
            for n in positions(count, group, here)
        ]
        panel = jnp.concatenate([piece[at].reshape(group * tile, tile) for piece in pieces], axis=0)
        part = jnp.dot(block(inverse, rows, cols), panel, preferred_element_type=F32)
        whole[at] = part.astype(BF16).reshape(per_row, tile, tile)


def near_kernel(
    nodes, choices, parent_two, order_two, own, sibling, ours, theirs, *refs
):
    here, chip, core = lax.axis_index(ROW), lax.axis_index(CHIP), lax.axis_index(CORE)
    inputs, (near, smalls, inverse, sems) = refs[: sum(choices)], refs[sum(choices) :]
    per_row, tile = near.shape[1], near.shape[2]
    copies = load(own, sibling, inverse, sems)
    is_end = jnp.logical_or(chip == 0, chip == nodes - 1)
    for t in range(nodes):
        mine, inputs = inputs[: choices[t]], inputs[choices[t] :]
        factor = mine[0][:per_row]
        if len(mine) > 1:
            factor = jnp.where(is_end, mine[1][:per_row], factor)
        node = 2 * (chip ^ t) + core
        parent = parent_two[node]
        is_ours = parent % 2 == core
        for m in range(per_row):
            at = order_two[node, here * per_row + m] - here * per_row
            near[t, m] = jnp.where(is_ours, ours[parent // 2, at], theirs[parent // 2, at])
        smalls[t] = lax.dot_general(
            near[t].reshape(per_row * tile, tile),
            factor.reshape(per_row * tile, tile),
            (((0,), (0,)), ((), ())),
            preferred_element_type=F32,
        ).astype(BF16)
    finish(copies)


def level_two_kernel(
    nodes, count, choices, rows_one, parent_two, order_two, inverse, near, upper, *refs
):
    here, chip, core = lax.axis_index(ROW), lax.axis_index(CHIP), lax.axis_index(CORE)
    pieces, refs = refs[:count], refs[count:]
    inputs, refs = refs[: sum(choices)], refs[sum(choices) :]
    columns, smalls = refs[:nodes], refs[nodes:]
    group, tile = pieces[0].shape[1], pieces[0].shape[2]
    per_row = group * count
    height, width = inverse.shape[1], 2 * inverse.shape[2]
    is_end = jnp.logical_or(chip == 0, chip == nodes - 1)
    factors = []
    for t in range(nodes):
        mine, inputs = inputs[: choices[t]], inputs[choices[t] :]
        factor = mine[0][...]
        if len(mine) > 1:
            factor = jnp.where(is_end, mine[1][...], factor)
        factors.append(factor[:per_row].reshape(per_row * tile, tile))
        node = 2 * (chip ^ t) + core
        parent = parent_two[node]
        rows = [
            rows_one[parent, order_two[node, here * per_row + m]] - here * height
            for m in range(per_row)
        ]
        cols = [
            rows_one[parent, order_two[node, chip * per_row + n]] - chip * width
            for n in positions(count, group, here)
        ]
        panel = [piece[chip ^ t].reshape(group * tile, tile) for piece in pieces]
        panel = jnp.concatenate(panel, axis=0)
        carried = jnp.dot(
            near[t].reshape(per_row * tile, tile), factor[per_row], preferred_element_type=F32
        )
        part = jnp.dot(block(inverse, rows, cols), panel, preferred_element_type=F32)
        columns[t][...] = (part - carried).astype(BF16).reshape(per_row, tile, tile)
        smalls[t][0] = upper[t]
    for t in range(nodes):
        smalls[t][1] = lax.dot_general(
            factors[t],
            columns[t][...].reshape(per_row * tile, tile),
            (((0,), (0,)), ((), ())),
            preferred_element_type=F32,
        ).astype(BF16)


def cut_kernel(panel, *outs):
    here = lax.axis_index(ROW)
    for s, out in enumerate(outs):
        group = out.shape[0]
        out[...] = panel[pl.ds(pl.multiple_of((here ^ s) * group, group), group)]


def cut_groups(panel, count):
    group = (panel.shape[0] // count,) + panel.shape[1:]
    return pl.pallas_call(
        cut_kernel,
        out_shape=[jax.ShapeDtypeStruct(group, BF16)] * count,
        in_specs=[VMEM],
        out_specs=[VMEM] * count,
        compiler_params=pltpu.CompilerParams(vmem_limit_bytes=LIMIT),
        name="cut_groups",
    )(panel)


def join_kernel(*refs):
    here = lax.axis_index(ROW)
    for s, ref in enumerate(refs[:-1]):
        refs[-1][here ^ s] = ref[...]


def join_groups(groups):
    return pl.pallas_call(
        join_kernel,
        out_shape=jax.ShapeDtypeStruct((len(groups),) + groups[0].shape, BF16),
        in_specs=[VMEM] * len(groups),
        out_specs=VMEM,
        compiler_params=pltpu.CompilerParams(vmem_limit_bytes=LIMIT),
        name="join_groups",
    )(*groups)


def column_kernel(parts, panel, *refs):
    smalls, (column, small) = refs[:-2], refs[-2:]
    column[...] = (-jnp.sum(parts[...].astype(F32), axis=0)).astype(BF16)
    shape = (panel.shape[0] * panel.shape[1], panel.shape[2])
    small[0] = lax.dot_general(
        panel[...].reshape(shape),
        column[...].reshape(shape),
        (((0,), (0,)), ((), ())),
        preferred_element_type=F32,
    ).astype(BF16)
    small[1:] = total([ref[...] for ref in smalls]).astype(BF16)


def form_column(parts, panel, smalls):
    return pl.pallas_call(
        column_kernel,
        out_shape=[
            jax.ShapeDtypeStruct(panel.shape, BF16),
            jax.ShapeDtypeStruct((3,) + panel.shape[1:], BF16),
        ],
        in_specs=[VMEM] * (2 + len(smalls)),
        out_specs=[VMEM] * 2,
        compiler_params=pltpu.CompilerParams(vmem_limit_bytes=LIMIT),
        name="form_column",
    )(parts, panel, *smalls)


def diagonal_kernel(base, *refs):
    parts, (diagonal, sums) = refs[:-2], refs[-2:]
    sums[...] = total([part[1:] for part in parts])
    diagonal[...] = (base[...] - total([part[0] for part in parts])).astype(BF16)


def form_diagonal(base, parts):
    return pl.pallas_call(
        diagonal_kernel,
        out_shape=[
            jax.ShapeDtypeStruct(base.shape, BF16),
            jax.ShapeDtypeStruct((2,) + base.shape, F32),
        ],
        in_specs=[VMEM] * (1 + len(parts)),
        out_specs=[VMEM] * 2,
        compiler_params=pltpu.CompilerParams(vmem_limit_bytes=LIMIT),
        name="form_diagonal",
    )(base, *parts)


def sum_kernel(*refs):
    refs[-1][...] = (-total([ref[...] for ref in refs[:-1]])).astype(BF16)


def form_sum(parts):
    return pl.pallas_call(
        sum_kernel,
        out_shape=jax.ShapeDtypeStruct(parts[0].shape, BF16),
        in_specs=[VMEM] * len(parts),
        out_specs=VMEM,
        compiler_params=pltpu.CompilerParams(vmem_limit_bytes=LIMIT),
        name="form_sum",
    )(*parts)


def choose_kernel(parent_two, ours, theirs, out):
    core = lax.axis_index(CORE)
    for at in range(out.shape[0]):
        out[at] = jnp.where(parent_two[2 * at + core] % 2 == core, ours[...], theirs[...])


def choose(nodes, parent_two, ours, theirs):
    return pl.pallas_call(
        choose_kernel,
        out_shape=jax.ShapeDtypeStruct((nodes,) + ours.shape, BF16),
        in_specs=[SMEM] + [VMEM] * 2,
        out_specs=VMEM,
        compiler_params=pltpu.CompilerParams(vmem_limit_bytes=LIMIT),
        name="choose",
    )(parent_two, ours, theirs)


def last_kernel(parent_two, link, base, diagonals, sums, upper, diagonal_two):
    chip, core = lax.axis_index(CHIP), lax.axis_index(CORE)
    near = diagonals[parent_two[2 * chip + core] // 2]
    parent_term = jnp.dot(near, link[...], preferred_element_type=F32)
    upper[...] = (sums[0] - parent_term).astype(BF16)
    term = lax.dot_general(
        link[...], upper[...], (((0,), (0,)), ((), ())), preferred_element_type=F32
    )
    diagonal_two[...] = (base[...] - term + sums[1]).astype(BF16)


def form_last(parent_two, link, base, diagonals, sums):
    return pl.pallas_call(
        last_kernel,
        out_shape=[jax.ShapeDtypeStruct(link.shape, BF16)] * 2,
        in_specs=[SMEM] + [VMEM] * 4,
        out_specs=[VMEM] * 2,
        compiler_params=pltpu.CompilerParams(vmem_limit_bytes=LIMIT),
        name="form_last",
    )(parent_two, link, base, diagonals, sums)


def level_one(rows_one, inverse, pieces):
    nodes, group, tile = pieces[0].shape[0], pieces[0].shape[1], pieces[0].shape[2]
    count = len(pieces)
    per_row = group * count
    flops = 2 * nodes * per_row * per_row * tile**3
    return pl.pallas_call(
        functools.partial(level_one_kernel, nodes, count),
        out_shape=jax.ShapeDtypeStruct((nodes, per_row, tile, tile), BF16),
        in_specs=[SMEM] + [VMEM] * (1 + count),
        out_specs=VMEM,
        compiler_params=pltpu.CompilerParams(vmem_limit_bytes=LIMIT),
        cost_estimate=pl.CostEstimate(flops=flops, bytes_accessed=12 << 20, transcendentals=0),
        name="level_one",
    )(rows_one, inverse, *pieces)


def form_near(parent_two, order_two, own, sibling, ours, theirs, factors):
    nodes, tiles = ours.shape[0], ours.shape[1:]
    choices = [len(f) for f in factors]
    return pl.pallas_call(
        functools.partial(near_kernel, nodes, choices),
        out_shape=[
            jax.ShapeDtypeStruct(ours.shape, BF16),
            jax.ShapeDtypeStruct((nodes,) + tiles[1:], BF16),
            jax.ShapeDtypeStruct((2,) + own.shape, BF16),
        ],
        in_specs=[SMEM] * 2 + [ANY] * 2 + [VMEM] * (2 + sum(choices)),
        out_specs=[VMEM] * 3,
        scratch_shapes=[pltpu.SemaphoreType.DMA((2 * PARTS,))],
        compiler_params=pltpu.CompilerParams(vmem_limit_bytes=LIMIT),
        name="form_near",
    )(parent_two, order_two, own, sibling, ours, theirs, *sum(factors, []))


def level_two(rows_one, parent_two, order_two, inverse, near, upper, pieces, factors):
    nodes, group, tile = pieces[0].shape[0], pieces[0].shape[1], pieces[0].shape[2]
    count = len(pieces)
    per_row = group * count
    flops = 2 * nodes * per_row * (per_row + 3) * tile**3
    choices = [len(f) for f in factors]
    return pl.pallas_call(
        functools.partial(level_two_kernel, nodes, count, choices),
        out_shape=[jax.ShapeDtypeStruct((per_row, tile, tile), BF16)] * nodes
        + [jax.ShapeDtypeStruct((2, tile, tile), BF16)] * nodes,
        in_specs=[SMEM] * 3 + [VMEM] * (3 + count + sum(choices)),
        out_specs=[VMEM] * (2 * nodes),
        compiler_params=pltpu.CompilerParams(vmem_limit_bytes=LIMIT),
        cost_estimate=pl.CostEstimate(flops=flops, bytes_accessed=16 << 20, transcendentals=0),
        name="level_two",
    )(rows_one, parent_two, order_two, inverse, near, upper, *pieces, *sum(factors, []))


def exchange(x, axis, step):
    size = lax.axis_size(axis)
    return lax.ppermute(x, axis, [(i, i ^ step) for i in range(size)])


def spread(x, axis):
    return [x] + [exchange(x, axis, s) for s in range(1, lax.axis_size(axis))]


def after(x, *others):
    return lax.optimization_barrier((x,) + others)[0]


def together(*arrays):
    return lax.optimization_barrier(arrays)


def halves(panel, axis):
    rows = lax.axis_size(axis)
    return panel.reshape((rows, panel.shape[0] // rows) + panel.shape[1:])


def swap(blocks, axis):
    return lax.all_to_all(blocks, axis, 0, 0, tiled=True)


def total(parts):
    return functools.reduce(jnp.add, [part.astype(F32) for part in parts])


def local(
    inverse_top, rows_one, panel_one, base_one, parent_two, order_two, panel_two, link_two, base_two
):
    chip, core = lax.axis_index(CHIP), lax.axis_index(CORE)
    nodes = lax.axis_size(CHIP)
    line = nodes == 4
    payload = jnp.concatenate([panel_two[0], link_two], axis=0)
    near = exchange(payload, CHIP, 1)
    if line:
        inner = lax.ppermute(payload, CHIP, [(1, 2), (2, 1)])
    else:
        inner = [exchange(payload, CHIP, t) for t in range(2, nodes)]
    sibling = exchange(inverse_top, CORE, 1)
    quarters = swap(halves(panel_one[0], ROW), ROW)
    kept, *sends = cut_groups(panel_two[0], lax.axis_size(ROW))
    quarters, near, inner, sends = together(quarters, near, inner, sends)
    blocks_one = swap(quarters, CHIP)
    groups = [kept] + [exchange(send, ROW, s + 1) for s, send in enumerate(sends)]
    blocks_one, groups = together(blocks_one, groups)
    quarters_two = join_groups(groups)
    pieces_one = spread(blocks_one, ROW)
    inverse = pair(inverse_top, after(sibling, blocks_one))
    quarters_two, payload_late, near_late, inner_late = together(
        quarters_two, payload, near, inner, blocks_one
    )[:4]
    blocks_two = swap(quarters_two, CHIP)
    over = out_one = ()
    if line:
        is_end = jnp.logical_or(chip == 0, chip == nodes - 1)
        over = exchange(jnp.where(is_end, payload_late, near_late), CHIP, nodes - 1)
        out_one = lax.ppermute(inner_late, CHIP, [(1, 0), (2, 3)])
    ours = level_one(rows_one, inverse, pieces_one)
    ours, blocks_two, over, out_one = together(ours, blocks_two, over, out_one)
    theirs = exchange(ours, CORE, 1)
    parts_one = swap(ours, CHIP)
    pieces_two = spread(blocks_two, ROW)
    if line:
        factors = [[payload], [near], [over, out_one], [inner, over]]
    else:
        factors = [[f] for f in [payload, near, *inner]]
    near_two, upper_part, inverse = form_near(
        parent_two, order_two, inverse_top, sibling, ours, theirs, factors
    )
    outs = level_two(
        rows_one, parent_two, order_two, inverse, near_two, upper_part, pieces_two, factors
    )
    columns, smalls = outs[:nodes], outs[nodes:]
    parts_small = [smalls[0]] + [exchange(smalls[t], CHIP, t) for t in range(1, nodes)]
    first = [exchange(columns[t], CHIP, t) for t in range(nodes // 2 + 1, nodes)]
    *columns, token = together(*columns, parts_small[1])
    parts_two = [exchange(columns[t], CHIP, t) for t in range(1, nodes // 2 + 1)] + first
    column_one, small = form_column(parts_one, panel_one[0], parts_small)
    diagonal_one, sums = form_diagonal(base_one[0], spread(small, ROW))
    chosen = choose(nodes, parent_two, diagonal_one, exchange(diagonal_one, CORE, 1))
    diagonals = swap(chosen, CHIP)
    upper, diagonal_two = form_last(parent_two, link_two[0], base_two[0], diagonals, sums)
    column_two = form_sum([columns[0], *parts_two])
    return (
        column_one[None],
        diagonal_one[None],
        column_two[None],
        upper[None],
        diagonal_two[None],
    )


def solution(mesh):
    rows, columns = mesh.devices.shape
    fine = Mesh(mesh.devices.reshape(rows, columns // 2, 2), (ROW, CHIP, CORE))
    col = (CHIP, CORE)
    return jax.shard_map(
        local,
        mesh=fine,
        in_specs=(
            P(ROW, col, None, None),
            P(),
            P(col, ROW, None, None),
            P(col, None, None),
            P(),
            P(),
            P(col, ROW, None, None),
            P(col, None, None),
            P(col, None, None),
        ),
        out_specs=(
            P(col, ROW, None, None),
            P(col, None, None),
            P(col, ROW, None, None),
            P(col, None, None),
            P(col, None, None),
        ),
        check_vma=False,
    )
```

```python
import functools

import jax
import jax.numpy as jnp
from jax import lax
from jax.experimental import pallas as pl
from jax.experimental.pallas import tpu as pltpu
from jax.sharding import Mesh, PartitionSpec as P

ROW, CHIP, CORE = "prow", "pchip", "pcore"
F32 = jnp.float32
BF16 = jnp.bfloat16
SMEM = pl.BlockSpec(memory_space=pltpu.SMEM)
VMEM = pl.BlockSpec(memory_space=pltpu.VMEM)
LIMIT = 24 << 20
PARTS = 4


HBM = pl.BlockSpec(memory_space=pltpu.HBM)
ANY = pl.BlockSpec(memory_space=pl.ANY)


def begin(copies):
    for copy in copies:
        copy.start()
    return copies


def finish(copies):
    for copy in copies:
        copy.wait()


def load(own, sibling, inverse, sems):
    core, step = lax.axis_index(CORE), own.shape[0] // PARTS
    copies = []
    for n in range(PARTS):
        rows = pl.ds(n * step, step)
        for k, (ref, at) in enumerate(((own, core), (sibling, 1 - core))):
            copies.append(
                pltpu.make_async_copy(ref.at[rows], inverse.at[at, rows], sems.at[2 * n + k])
            )
    return begin(copies)


def pair_kernel(own, sibling, inverse, sems):
    finish(load(own, sibling, inverse, sems))


def pair(own, sibling):
    return pl.pallas_call(
        pair_kernel,
        out_shape=jax.ShapeDtypeStruct((2,) + own.shape, BF16),
        in_specs=[ANY] * 2,
        out_specs=VMEM,
        scratch_shapes=[pltpu.SemaphoreType.DMA((2 * PARTS,))],
        compiler_params=pltpu.CompilerParams(vmem_limit_bytes=LIMIT),
        name="pair",
    )(own, sibling)


def positions(count, group, here):
    return [(here ^ s) * group + g for s in range(count) for g in range(group)]


def block(inverse, rows, cols):
    width = inverse.shape[2]
    lines = []
    for row in rows:
        tiles = [inverse[col // width, row, col % width] for col in cols]
        lines.append(jnp.concatenate(tiles, axis=1))
    return jnp.concatenate(lines, axis=0)


def level_one_kernel(nodes, count, rows_one, inverse, *refs):
    here, chip, core = lax.axis_index(ROW), lax.axis_index(CHIP), lax.axis_index(CORE)
    pieces, whole = refs[:count], refs[count]
    group, tile = pieces[0].shape[1], pieces[0].shape[2]
    per_row = group * count
    height, width = inverse.shape[1], 2 * inverse.shape[2]
    for at in range(nodes):
        node = 2 * at + core
        rows = [rows_one[node, here * per_row + m] - here * height for m in range(per_row)]
        cols = [
            rows_one[node, chip * per_row + n] - chip * width
            for n in positions(count, group, here)
        ]
        panel = jnp.concatenate([piece[at].reshape(group * tile, tile) for piece in pieces], axis=0)
        part = jnp.dot(block(inverse, rows, cols), panel, preferred_element_type=F32)
        whole[at] = part.astype(BF16).reshape(per_row, tile, tile)


def near_kernel(
    nodes, choices, parent_two, order_two, own, sibling, ours, theirs, *refs
):
    here, chip, core = lax.axis_index(ROW), lax.axis_index(CHIP), lax.axis_index(CORE)
    inputs, (near, smalls, inverse, sems) = refs[: sum(choices)], refs[sum(choices) :]
    per_row, tile = near.shape[1], near.shape[2]
    copies = load(own, sibling, inverse, sems)
    is_end = jnp.logical_or(chip == 0, chip == nodes - 1)
    for t in range(nodes):
        mine, inputs = inputs[: choices[t]], inputs[choices[t] :]
        factor = mine[0][:per_row]
        if len(mine) > 1:
            factor = jnp.where(is_end, mine[1][:per_row], factor)
        node = 2 * (chip ^ t) + core
        parent = parent_two[node]
        is_ours = parent % 2 == core
        for m in range(per_row):
            at = order_two[node, here * per_row + m] - here * per_row
            near[t, m] = jnp.where(is_ours, ours[parent // 2, at], theirs[parent // 2, at])
        smalls[t] = lax.dot_general(
            near[t].reshape(per_row * tile, tile),
            factor.reshape(per_row * tile, tile),
            (((0,), (0,)), ((), ())),
            preferred_element_type=F32,
        ).astype(BF16)
    finish(copies)


def level_two_kernel(
    nodes, count, choices, rows_one, parent_two, order_two, inverse, near, upper, *refs
):
    here, chip, core = lax.axis_index(ROW), lax.axis_index(CHIP), lax.axis_index(CORE)
    pieces, refs = refs[:count], refs[count:]
    inputs, refs = refs[: sum(choices)], refs[sum(choices) :]
    columns, smalls = refs[:nodes], refs[nodes:]
    group, tile = pieces[0].shape[1], pieces[0].shape[2]
    per_row = group * count
    height, width = inverse.shape[1], 2 * inverse.shape[2]
    is_end = jnp.logical_or(chip == 0, chip == nodes - 1)
    factors = []
    for t in range(nodes):
        mine, inputs = inputs[: choices[t]], inputs[choices[t] :]
        factor = mine[0][...]
        if len(mine) > 1:
            factor = jnp.where(is_end, mine[1][...], factor)
        factors.append(factor[:per_row].reshape(per_row * tile, tile))
        node = 2 * (chip ^ t) + core
        parent = parent_two[node]
        rows = [
            rows_one[parent, order_two[node, here * per_row + m]] - here * height
            for m in range(per_row)
        ]
        cols = [
            rows_one[parent, order_two[node, chip * per_row + n]] - chip * width
            for n in positions(count, group, here)
        ]
        panel = [piece[chip ^ t].reshape(group * tile, tile) for piece in pieces]
        panel = jnp.concatenate(panel, axis=0)
        carried = jnp.dot(
            near[t].reshape(per_row * tile, tile), factor[per_row], preferred_element_type=F32
        )
        part = jnp.dot(block(inverse, rows, cols), panel, preferred_element_type=F32)
        columns[t][...] = (part - carried).astype(BF16).reshape(per_row, tile, tile)
        smalls[t][0] = upper[t]
    for t in range(nodes):
        smalls[t][1] = lax.dot_general(
            factors[t],
            columns[t][...].reshape(per_row * tile, tile),
            (((0,), (0,)), ((), ())),
            preferred_element_type=F32,
        ).astype(BF16)


def cut_kernel(panel, *outs):
    here = lax.axis_index(ROW)
    for s, out in enumerate(outs):
        group = out.shape[0]
        out[...] = panel[pl.ds(pl.multiple_of((here ^ s) * group, group), group)]


def cut_groups(panel, count):
    group = (panel.shape[0] // count,) + panel.shape[1:]
    return pl.pallas_call(
        cut_kernel,
        out_shape=[jax.ShapeDtypeStruct(group, BF16)] * count,
        in_specs=[VMEM],
        out_specs=[VMEM] * count,
        compiler_params=pltpu.CompilerParams(vmem_limit_bytes=LIMIT),
        name="cut_groups",
    )(panel)


def join_kernel(*refs):
    here = lax.axis_index(ROW)
    for s, ref in enumerate(refs[:-1]):
        refs[-1][here ^ s] = ref[...]


def join_groups(groups):
    return pl.pallas_call(
        join_kernel,
        out_shape=jax.ShapeDtypeStruct((len(groups),) + groups[0].shape, BF16),
        in_specs=[VMEM] * len(groups),
        out_specs=VMEM,
        compiler_params=pltpu.CompilerParams(vmem_limit_bytes=LIMIT),
        name="join_groups",
    )(*groups)


def column_kernel(parts, panel, column, part):
    column[...] = (-jnp.sum(parts[...].astype(F32), axis=0)).astype(BF16)
    shape = (panel.shape[0] * panel.shape[1], panel.shape[2])
    part[...] = lax.dot_general(
        panel[...].reshape(shape),
        column[...].reshape(shape),
        (((0,), (0,)), ((), ())),
        preferred_element_type=F32,
    ).astype(BF16)


def form_column(parts, panel):
    return pl.pallas_call(
        column_kernel,
        out_shape=[
            jax.ShapeDtypeStruct(panel.shape, BF16),
            jax.ShapeDtypeStruct(panel.shape[1:], BF16),
        ],
        in_specs=[VMEM] * 2,
        out_specs=[VMEM] * 2,
        compiler_params=pltpu.CompilerParams(vmem_limit_bytes=LIMIT),
        name="form_column",
    )(parts, panel)


def sum_kernel(*refs):
    refs[-1][...] = (-total([ref[...] for ref in refs[:-1]])).astype(BF16)


def form_sum(parts):
    return pl.pallas_call(
        sum_kernel,
        out_shape=jax.ShapeDtypeStruct(parts[0].shape, BF16),
        in_specs=[VMEM] * len(parts),
        out_specs=VMEM,
        compiler_params=pltpu.CompilerParams(vmem_limit_bytes=LIMIT),
        name="form_sum",
    )(*parts)


def choose_kernel(nodes, parent_two, ours, theirs, *outs):
    chip, core = lax.axis_index(CHIP), lax.axis_index(CORE)
    for t in range(nodes):
        parent = parent_two[2 * (chip ^ t) + core]
        outs[t][...] = jnp.where(parent % 2 == core, ours[...], theirs[...])


def choose(nodes, parent_two, ours, theirs):
    return pl.pallas_call(
        functools.partial(choose_kernel, nodes),
        out_shape=[jax.ShapeDtypeStruct(ours.shape, BF16)] * nodes,
        in_specs=[SMEM] + [VMEM] * 2,
        out_specs=[VMEM] * nodes,
        compiler_params=pltpu.CompilerParams(vmem_limit_bytes=LIMIT),
        name="choose",
    )(parent_two, ours, theirs)


def last_kernel(nodes, parent_two, link, base, *refs):
    diagonals, parts, (upper, diagonal_two) = refs[:nodes], refs[nodes:-2], refs[-2:]
    chip, core = lax.axis_index(CHIP), lax.axis_index(CORE)
    step = (parent_two[2 * chip + core] // 2) ^ chip
    near = diagonals[0][...]
    for t in range(1, nodes):
        near = jnp.where(step == t, diagonals[t][...], near)
    sums = total([part[...] for part in parts])
    parent_term = jnp.dot(near, link[...], preferred_element_type=F32)
    upper[...] = (sums[0] - parent_term).astype(BF16)
    term = lax.dot_general(
        link[...], upper[...], (((0,), (0,)), ((), ())), preferred_element_type=F32
    )
    diagonal_two[...] = (base[...] - term + sums[1]).astype(BF16)


def form_last(parent_two, link, base, diagonals, parts):
    return pl.pallas_call(
        functools.partial(last_kernel, len(diagonals)),
        out_shape=[jax.ShapeDtypeStruct(link.shape, BF16)] * 2,
        in_specs=[SMEM] + [VMEM] * (2 + len(diagonals) + len(parts)),
        out_specs=[VMEM] * 2,
        compiler_params=pltpu.CompilerParams(vmem_limit_bytes=LIMIT),
        name="form_last",
    )(parent_two, link, base, *diagonals, *parts)


def level_one(rows_one, inverse, pieces):
    nodes, group, tile = pieces[0].shape[0], pieces[0].shape[1], pieces[0].shape[2]
    count = len(pieces)
    per_row = group * count
    flops = 2 * nodes * per_row * per_row * tile**3
    return pl.pallas_call(
        functools.partial(level_one_kernel, nodes, count),
        out_shape=jax.ShapeDtypeStruct((nodes, per_row, tile, tile), BF16),
        in_specs=[SMEM] + [VMEM] * (1 + count),
        out_specs=VMEM,
        compiler_params=pltpu.CompilerParams(vmem_limit_bytes=LIMIT),
        cost_estimate=pl.CostEstimate(flops=flops, bytes_accessed=12 << 20, transcendentals=0),
        name="level_one",
    )(rows_one, inverse, *pieces)


def form_near(parent_two, order_two, own, sibling, ours, theirs, factors):
    nodes, tiles = ours.shape[0], ours.shape[1:]
    choices = [len(f) for f in factors]
    return pl.pallas_call(
        functools.partial(near_kernel, nodes, choices),
        out_shape=[
            jax.ShapeDtypeStruct(ours.shape, BF16),
            jax.ShapeDtypeStruct((nodes,) + tiles[1:], BF16),
            jax.ShapeDtypeStruct((2,) + own.shape, BF16),
        ],
        in_specs=[SMEM] * 2 + [ANY] * 2 + [VMEM] * (2 + sum(choices)),
        out_specs=[VMEM] * 3,
        scratch_shapes=[pltpu.SemaphoreType.DMA((2 * PARTS,))],
        compiler_params=pltpu.CompilerParams(vmem_limit_bytes=LIMIT),
        name="form_near",
    )(parent_two, order_two, own, sibling, ours, theirs, *sum(factors, []))


def level_two(rows_one, parent_two, order_two, inverse, near, upper, pieces, factors):
    nodes, group, tile = pieces[0].shape[0], pieces[0].shape[1], pieces[0].shape[2]
    count = len(pieces)
    per_row = group * count
    flops = 2 * nodes * per_row * (per_row + 3) * tile**3
    choices = [len(f) for f in factors]
    return pl.pallas_call(
        functools.partial(level_two_kernel, nodes, count, choices),
        out_shape=[jax.ShapeDtypeStruct((per_row, tile, tile), BF16)] * nodes
        + [jax.ShapeDtypeStruct((2, tile, tile), BF16)] * nodes,
        in_specs=[SMEM] * 3 + [VMEM] * (3 + count + sum(choices)),
        out_specs=[VMEM] * (2 * nodes),
        compiler_params=pltpu.CompilerParams(vmem_limit_bytes=LIMIT),
        cost_estimate=pl.CostEstimate(flops=flops, bytes_accessed=16 << 20, transcendentals=0),
        name="level_two",
    )(rows_one, parent_two, order_two, inverse, near, upper, *pieces, *sum(factors, []))


def exchange(x, axis, step):
    size = lax.axis_size(axis)
    return lax.ppermute(x, axis, [(i, i ^ step) for i in range(size)])


def spread(x, axis):
    return [x] + [exchange(x, axis, s) for s in range(1, lax.axis_size(axis))]


def after(x, *others):
    return lax.optimization_barrier((x,) + others)[0]


def together(*arrays):
    return lax.optimization_barrier(arrays)


def halves(panel, axis):
    rows = lax.axis_size(axis)
    return panel.reshape((rows, panel.shape[0] // rows) + panel.shape[1:])


def swap(blocks, axis):
    return lax.all_to_all(blocks, axis, 0, 0, tiled=True)


def total(parts):
    return functools.reduce(jnp.add, [part.astype(F32) for part in parts])


def local(
    inverse_top, rows_one, panel_one, base_one, parent_two, order_two, panel_two, link_two, base_two
):
    chip, core = lax.axis_index(CHIP), lax.axis_index(CORE)
    nodes = lax.axis_size(CHIP)
    line = nodes == 4
    payload = jnp.concatenate([panel_two[0], link_two], axis=0)
    near = exchange(payload, CHIP, 1)
    if line:
        inner = lax.ppermute(payload, CHIP, [(1, 2), (2, 1)])
    else:
        inner = [exchange(payload, CHIP, t) for t in range(2, nodes)]
    sibling = exchange(inverse_top, CORE, 1)
    quarters = swap(halves(panel_one[0], ROW), ROW)
    kept, *sends = cut_groups(panel_two[0], lax.axis_size(ROW))
    quarters, near, inner, sends = together(quarters, near, inner, sends)
    blocks_one = swap(quarters, CHIP)
    groups = [kept] + [exchange(send, ROW, s + 1) for s, send in enumerate(sends)]
    blocks_one, groups = together(blocks_one, groups)
    quarters_two = join_groups(groups)
    pieces_one = spread(blocks_one, ROW)
    inverse = pair(inverse_top, after(sibling, blocks_one))
    quarters_two, payload_late, near_late, inner_late = together(
        quarters_two, payload, near, inner, blocks_one
    )[:4]
    blocks_two = swap(quarters_two, CHIP)
    over = out_one = ()
    if line:
        is_end = jnp.logical_or(chip == 0, chip == nodes - 1)
        over = exchange(jnp.where(is_end, payload_late, near_late), CHIP, nodes - 1)
        out_one = lax.ppermute(inner_late, CHIP, [(1, 0), (2, 3)])
    ours = level_one(rows_one, inverse, pieces_one)
    ours, blocks_two, over, out_one = together(ours, blocks_two, over, out_one)
    theirs = exchange(ours, CORE, 1)
    parts_one = swap(ours, CHIP)
    pieces_two = spread(blocks_two, ROW)
    if line:
        factors = [[payload], [near], [over, out_one], [inner, over]]
    else:
        factors = [[f] for f in [payload, near, *inner]]
    near_two, upper_part, inverse = form_near(
        parent_two, order_two, inverse_top, sibling, ours, theirs, factors
    )
    outs = level_two(
        rows_one, parent_two, order_two, inverse, near_two, upper_part, pieces_two, factors
    )
    columns, smalls = outs[:nodes], outs[nodes:]
    parts_small = [smalls[0]] + [exchange(smalls[t], CHIP, t) for t in range(1, nodes)]
    first = [exchange(columns[t], CHIP, t) for t in range(nodes // 2 + 1, nodes)]
    column_one, part = form_column(parts_one, panel_one[0])
    columns, parts_small, parts_diagonal = together(columns, parts_small, spread(part, ROW))
    parts_two = [exchange(columns[t], CHIP, t) for t in range(1, nodes // 2 + 1)] + first
    diagonal_one = (base_one[0] - total(parts_diagonal)).astype(BF16)
    chosen = choose(nodes, parent_two, diagonal_one, exchange(diagonal_one, CORE, 1))
    diagonals = [chosen[0]] + [exchange(chosen[t], CHIP, t) for t in range(1, nodes)]
    parts_last = spread(total(parts_small).astype(BF16), ROW)
    upper, diagonal_two = form_last(parent_two, link_two[0], base_two[0], diagonals, parts_last)
    column_two = form_sum([columns[0], *parts_two])
    return (
        column_one[None],
        diagonal_one[None],
        column_two[None],
        upper[None],
        diagonal_two[None],
    )


def solution(mesh):
    rows, columns = mesh.devices.shape
    fine = Mesh(mesh.devices.reshape(rows, columns // 2, 2), (ROW, CHIP, CORE))
    col = (CHIP, CORE)
    return jax.shard_map(
        local,
        mesh=fine,
        in_specs=(
            P(ROW, col, None, None),
            P(),
            P(col, ROW, None, None),
            P(col, None, None),
            P(),
            P(),
            P(col, ROW, None, None),
            P(col, None, None),
            P(col, None, None),
        ),
        out_specs=(
            P(col, ROW, None, None),
            P(col, None, None),
            P(col, ROW, None, None),
            P(col, None, None),
            P(col, None, None),
        ),
        check_vma=False,
    )
```

```python
import functools

import jax
import jax.numpy as jnp
from jax import lax
from jax.experimental import pallas as pl
from jax.experimental.pallas import tpu as pltpu
from jax.sharding import Mesh, PartitionSpec as P

ROW, CHIP, CORE = "prow", "pchip", "pcore"
F32 = jnp.float32
BF16 = jnp.bfloat16
SMEM = pl.BlockSpec(memory_space=pltpu.SMEM)
VMEM = pl.BlockSpec(memory_space=pltpu.VMEM)
LIMIT = 24 << 20
PARTS = 4


HBM = pl.BlockSpec(memory_space=pltpu.HBM)
ANY = pl.BlockSpec(memory_space=pl.ANY)


def begin(copies):
    for copy in copies:
        copy.start()
    return copies


def finish(copies):
    for copy in copies:
        copy.wait()


def load(own, sibling, inverse, sems):
    core, step = lax.axis_index(CORE), own.shape[0] // PARTS
    copies = []
    for n in range(PARTS):
        rows = pl.ds(n * step, step)
        for k, (ref, at) in enumerate(((own, core), (sibling, 1 - core))):
            copies.append(
                pltpu.make_async_copy(ref.at[rows], inverse.at[at, rows], sems.at[2 * n + k])
            )
    return begin(copies)


def pair_kernel(own, sibling, inverse, sems):
    finish(load(own, sibling, inverse, sems))


def pair(own, sibling):
    return pl.pallas_call(
        pair_kernel,
        out_shape=jax.ShapeDtypeStruct((2,) + own.shape, BF16),
        in_specs=[ANY] * 2,
        out_specs=VMEM,
        scratch_shapes=[pltpu.SemaphoreType.DMA((2 * PARTS,))],
        compiler_params=pltpu.CompilerParams(vmem_limit_bytes=LIMIT),
        name="pair",
    )(own, sibling)


def positions(count, group, here):
    return [(here ^ s) * group + g for s in range(count) for g in range(group)]


def block(inverse, rows, cols):
    width = inverse.shape[2]
    lines = []
    for row in rows:
        tiles = [inverse[col // width, row, col % width] for col in cols]
        lines.append(jnp.concatenate(tiles, axis=1))
    return jnp.concatenate(lines, axis=0)


def level_one_kernel(nodes, count, rows_one, inverse, *refs):
    here, chip, core = lax.axis_index(ROW), lax.axis_index(CHIP), lax.axis_index(CORE)
    pieces, whole = refs[:count], refs[count]
    group, tile = pieces[0].shape[1], pieces[0].shape[2]
    per_row = group * count
    height, width = inverse.shape[1], 2 * inverse.shape[2]
    for at in range(nodes):
        node = 2 * at + core
        rows = [rows_one[node, here * per_row + m] - here * height for m in range(per_row)]
        cols = [
            rows_one[node, chip * per_row + n] - chip * width
            for n in positions(count, group, here)
        ]
        panel = jnp.concatenate([piece[at].reshape(group * tile, tile) for piece in pieces], axis=0)
        part = jnp.dot(block(inverse, rows, cols), panel, preferred_element_type=F32)
        whole[at] = part.astype(BF16).reshape(per_row, tile, tile)


def near_kernel(
    nodes, choices, parent_two, order_two, own, sibling, ours, theirs, *refs
):
    here, chip, core = lax.axis_index(ROW), lax.axis_index(CHIP), lax.axis_index(CORE)
    inputs, (near, smalls, inverse, sems) = refs[: sum(choices)], refs[sum(choices) :]
    per_row, tile = near.shape[1], near.shape[2]
    copies = load(own, sibling, inverse, sems)
    is_end = jnp.logical_or(chip == 0, chip == nodes - 1)
    for t in range(nodes):
        mine, inputs = inputs[: choices[t]], inputs[choices[t] :]
        factor = mine[0][:per_row]
        if len(mine) > 1:
            factor = jnp.where(is_end, mine[1][:per_row], factor)
        node = 2 * (chip ^ t) + core
        parent = parent_two[node]
        is_ours = parent % 2 == core
        for m in range(per_row):
            at = order_two[node, here * per_row + m] - here * per_row
            near[t, m] = jnp.where(is_ours, ours[parent // 2, at], theirs[parent // 2, at])
        smalls[t] = lax.dot_general(
            near[t].reshape(per_row * tile, tile),
            factor.reshape(per_row * tile, tile),
            (((0,), (0,)), ((), ())),
            preferred_element_type=F32,
        ).astype(BF16)
    finish(copies)


def level_two_kernel(
    nodes, count, choices, rows_one, parent_two, order_two, inverse, near, upper, *refs
):
    here, chip, core = lax.axis_index(ROW), lax.axis_index(CHIP), lax.axis_index(CORE)
    pieces, refs = refs[:count], refs[count:]
    inputs, refs = refs[: sum(choices)], refs[sum(choices) :]
    columns, smalls = refs[:nodes], refs[nodes:]
    group, tile = pieces[0].shape[1], pieces[0].shape[2]
    per_row = group * count
    height, width = inverse.shape[1], 2 * inverse.shape[2]
    is_end = jnp.logical_or(chip == 0, chip == nodes - 1)
    factors = []
    for t in range(nodes):
        mine, inputs = inputs[: choices[t]], inputs[choices[t] :]
        factor = mine[0][...]
        if len(mine) > 1:
            factor = jnp.where(is_end, mine[1][...], factor)
        factors.append(factor[:per_row].reshape(per_row * tile, tile))
        node = 2 * (chip ^ t) + core
        parent = parent_two[node]
        rows = [
            rows_one[parent, order_two[node, here * per_row + m]] - here * height
            for m in range(per_row)
        ]
        cols = [
            rows_one[parent, order_two[node, chip * per_row + n]] - chip * width
            for n in positions(count, group, here)
        ]
        panel = [piece[chip ^ t].reshape(group * tile, tile) for piece in pieces]
        panel = jnp.concatenate(panel, axis=0)
        carried = jnp.dot(
            near[t].reshape(per_row * tile, tile), factor[per_row], preferred_element_type=F32
        )
        part = jnp.dot(block(inverse, rows, cols), panel, preferred_element_type=F32)
        columns[t][...] = (part - carried).astype(BF16).reshape(per_row, tile, tile)
        smalls[t][0] = upper[t]
    for t in range(nodes):
        smalls[t][1] = lax.dot_general(
            factors[t],
            columns[t][...].reshape(per_row * tile, tile),
            (((0,), (0,)), ((), ())),
            preferred_element_type=F32,
        ).astype(BF16)


def cut_kernel(panel, *outs):
    here = lax.axis_index(ROW)
    for s, out in enumerate(outs):
        group = out.shape[0]
        out[...] = panel[pl.ds(pl.multiple_of((here ^ s) * group, group), group)]


def cut_groups(panel, count):
    group = (panel.shape[0] // count,) + panel.shape[1:]
    return pl.pallas_call(
        cut_kernel,
        out_shape=[jax.ShapeDtypeStruct(group, BF16)] * count,
        in_specs=[VMEM],
        out_specs=[VMEM] * count,
        compiler_params=pltpu.CompilerParams(vmem_limit_bytes=LIMIT),
        name="cut_groups",
    )(panel)


def join_kernel(*refs):
    here = lax.axis_index(ROW)
    for s, ref in enumerate(refs[:-1]):
        refs[-1][here ^ s] = ref[...]


def join_groups(groups):
    return pl.pallas_call(
        join_kernel,
        out_shape=jax.ShapeDtypeStruct((len(groups),) + groups[0].shape, BF16),
        in_specs=[VMEM] * len(groups),
        out_specs=VMEM,
        compiler_params=pltpu.CompilerParams(vmem_limit_bytes=LIMIT),
        name="join_groups",
    )(*groups)


def column_kernel(parts, panel, column, part):
    column[...] = (-jnp.sum(parts[...].astype(F32), axis=0)).astype(BF16)
    shape = (panel.shape[0] * panel.shape[1], panel.shape[2])
    part[...] = lax.dot_general(
        panel[...].reshape(shape),
        column[...].reshape(shape),
        (((0,), (0,)), ((), ())),
        preferred_element_type=F32,
    ).astype(BF16)


def form_column(parts, panel):
    return pl.pallas_call(
        column_kernel,
        out_shape=[
            jax.ShapeDtypeStruct(panel.shape, BF16),
            jax.ShapeDtypeStruct(panel.shape[1:], BF16),
        ],
        in_specs=[VMEM] * 2,
        out_specs=[VMEM] * 2,
        compiler_params=pltpu.CompilerParams(vmem_limit_bytes=LIMIT),
        name="form_column",
    )(parts, panel)


def sum_kernel(*refs):
    refs[-1][...] = (-total([ref[...] for ref in refs[:-1]])).astype(BF16)


def form_sum(parts):
    return pl.pallas_call(
        sum_kernel,
        out_shape=jax.ShapeDtypeStruct(parts[0].shape, BF16),
        in_specs=[VMEM] * len(parts),
        out_specs=VMEM,
        compiler_params=pltpu.CompilerParams(vmem_limit_bytes=LIMIT),
        name="form_sum",
    )(*parts)


def choose_kernel(nodes, parent_two, ours, theirs, *outs):
    chip, core = lax.axis_index(CHIP), lax.axis_index(CORE)
    for t in range(nodes):
        parent = parent_two[2 * (chip ^ t) + core]
        outs[t][...] = jnp.where(parent % 2 == core, ours[...], theirs[...])


def choose(nodes, parent_two, ours, theirs):
    return pl.pallas_call(
        functools.partial(choose_kernel, nodes),
        out_shape=[jax.ShapeDtypeStruct(ours.shape, BF16)] * nodes,
        in_specs=[SMEM] + [VMEM] * 2,
        out_specs=[VMEM] * nodes,
        compiler_params=pltpu.CompilerParams(vmem_limit_bytes=LIMIT),
        name="choose",
    )(parent_two, ours, theirs)


def last_kernel(nodes, parent_two, link, base, *refs):
    diagonals, parts, (upper, diagonal_two) = refs[:nodes], refs[nodes:-2], refs[-2:]
    chip, core = lax.axis_index(CHIP), lax.axis_index(CORE)
    step = (parent_two[2 * chip + core] // 2) ^ chip
    near = diagonals[0][...]
    for t in range(1, nodes):
        near = jnp.where(step == t, diagonals[t][...], near)
    sums = total([part[...] for part in parts])
    parent_term = jnp.dot(near, link[...], preferred_element_type=F32)
    upper[...] = (sums[0] - parent_term).astype(BF16)
    term = lax.dot_general(
        link[...], upper[...], (((0,), (0,)), ((), ())), preferred_element_type=F32
    )
    diagonal_two[...] = (base[...] - term + sums[1]).astype(BF16)


def form_last(parent_two, link, base, diagonals, parts):
    return pl.pallas_call(
        functools.partial(last_kernel, len(diagonals)),
        out_shape=[jax.ShapeDtypeStruct(link.shape, BF16)] * 2,
        in_specs=[SMEM] + [VMEM] * (2 + len(diagonals) + len(parts)),
        out_specs=[VMEM] * 2,
        compiler_params=pltpu.CompilerParams(vmem_limit_bytes=LIMIT),
        name="form_last",
    )(parent_two, link, base, *diagonals, *parts)


def level_one(rows_one, inverse, pieces):
    nodes, group, tile = pieces[0].shape[0], pieces[0].shape[1], pieces[0].shape[2]
    count = len(pieces)
    per_row = group * count
    flops = 2 * nodes * per_row * per_row * tile**3
    return pl.pallas_call(
        functools.partial(level_one_kernel, nodes, count),
        out_shape=jax.ShapeDtypeStruct((nodes, per_row, tile, tile), BF16),
        in_specs=[SMEM] + [VMEM] * (1 + count),
        out_specs=VMEM,
        compiler_params=pltpu.CompilerParams(vmem_limit_bytes=LIMIT),
        cost_estimate=pl.CostEstimate(flops=flops, bytes_accessed=12 << 20, transcendentals=0),
        name="level_one",
    )(rows_one, inverse, *pieces)


def form_near(parent_two, order_two, own, sibling, ours, theirs, factors):
    nodes, tiles = ours.shape[0], ours.shape[1:]
    choices = [len(f) for f in factors]
    return pl.pallas_call(
        functools.partial(near_kernel, nodes, choices),
        out_shape=[
            jax.ShapeDtypeStruct(ours.shape, BF16),
            jax.ShapeDtypeStruct((nodes,) + tiles[1:], BF16),
            jax.ShapeDtypeStruct((2,) + own.shape, BF16),
        ],
        in_specs=[SMEM] * 2 + [ANY] * 2 + [VMEM] * (2 + sum(choices)),
        out_specs=[VMEM] * 3,
        scratch_shapes=[pltpu.SemaphoreType.DMA((2 * PARTS,))],
        compiler_params=pltpu.CompilerParams(vmem_limit_bytes=LIMIT),
        name="form_near",
    )(parent_two, order_two, own, sibling, ours, theirs, *sum(factors, []))


def level_two(rows_one, parent_two, order_two, inverse, near, upper, pieces, factors):
    nodes, group, tile = pieces[0].shape[0], pieces[0].shape[1], pieces[0].shape[2]
    count = len(pieces)
    per_row = group * count
    flops = 2 * nodes * per_row * (per_row + 3) * tile**3
    choices = [len(f) for f in factors]
    return pl.pallas_call(
        functools.partial(level_two_kernel, nodes, count, choices),
        out_shape=[jax.ShapeDtypeStruct((per_row, tile, tile), BF16)] * nodes
        + [jax.ShapeDtypeStruct((2, tile, tile), BF16)] * nodes,
        in_specs=[SMEM] * 3 + [VMEM] * (3 + count + sum(choices)),
        out_specs=[VMEM] * (2 * nodes),
        compiler_params=pltpu.CompilerParams(vmem_limit_bytes=LIMIT),
        cost_estimate=pl.CostEstimate(flops=flops, bytes_accessed=16 << 20, transcendentals=0),
        name="level_two",
    )(rows_one, parent_two, order_two, inverse, near, upper, *pieces, *sum(factors, []))


def exchange(x, axis, step):
    size = lax.axis_size(axis)
    return lax.ppermute(x, axis, [(i, i ^ step) for i in range(size)])


def spread(x, axis):
    return [x] + [exchange(x, axis, s) for s in range(1, lax.axis_size(axis))]


def after(x, *others):
    return lax.optimization_barrier((x,) + others)[0]


def together(*arrays):
    return lax.optimization_barrier(arrays)


def halves(panel, axis):
    rows = lax.axis_size(axis)
    return panel.reshape((rows, panel.shape[0] // rows) + panel.shape[1:])


def swap(blocks, axis):
    return lax.all_to_all(blocks, axis, 0, 0, tiled=True)


def total(parts):
    return functools.reduce(jnp.add, [part.astype(F32) for part in parts])


def local(
    inverse_top, rows_one, panel_one, base_one, parent_two, order_two, panel_two, link_two, base_two
):
    chip, core = lax.axis_index(CHIP), lax.axis_index(CORE)
    nodes = lax.axis_size(CHIP)
    line = nodes == 4
    payload = jnp.concatenate([panel_two[0], link_two], axis=0)
    near = exchange(payload, CHIP, 1)
    if line:
        inner = lax.ppermute(payload, CHIP, [(1, 2), (2, 1)])
    else:
        inner = [exchange(payload, CHIP, t) for t in range(2, nodes)]
    sibling = exchange(inverse_top, CORE, 1)
    quarters = swap(halves(panel_one[0], ROW), ROW)
    kept, *sends = cut_groups(panel_two[0], lax.axis_size(ROW))
    quarters, near, inner, sends = together(quarters, near, inner, sends)
    blocks_one = swap(quarters, CHIP)
    groups = [kept] + [exchange(send, ROW, s + 1) for s, send in enumerate(sends)]
    quarters_two = join_groups(groups)
    pieces_one = spread(blocks_one, ROW)
    inverse = pair(inverse_top, after(sibling, blocks_one))
    quarters_two, payload_late, near_late, inner_late = together(
        quarters_two, payload, near, inner, blocks_one
    )[:4]
    blocks_two = swap(quarters_two, CHIP)
    over = out_one = ()
    if line:
        is_end = jnp.logical_or(chip == 0, chip == nodes - 1)
        over = exchange(jnp.where(is_end, payload_late, near_late), CHIP, nodes - 1)
        out_one = lax.ppermute(inner_late, CHIP, [(1, 0), (2, 3)])
    ours = level_one(rows_one, inverse, pieces_one)
    ours, blocks_two, over, out_one = together(ours, blocks_two, over, out_one)
    theirs = exchange(ours, CORE, 1)
    parts_one = swap(ours, CHIP)
    pieces_two = spread(blocks_two, ROW)
    if line:
        factors = [[payload], [near], [over, out_one], [inner, over]]
    else:
        factors = [[f] for f in [payload, near, *inner]]
    near_two, upper_part, inverse = form_near(
        parent_two, order_two, inverse_top, sibling, ours, theirs, factors
    )
    outs = level_two(
        rows_one, parent_two, order_two, inverse, near_two, upper_part, pieces_two, factors
    )
    columns, smalls = outs[:nodes], outs[nodes:]
    parts_small = [smalls[0]] + [exchange(smalls[t], CHIP, t) for t in range(1, nodes)]
    first = [exchange(columns[t], CHIP, t) for t in range(nodes // 2, nodes)]
    column_one, part = form_column(parts_one, panel_one[0])
    columns, parts_small, parts_diagonal = together(columns, parts_small, spread(part, ROW))
    parts_two = [exchange(columns[t], CHIP, t) for t in range(1, nodes // 2)] + first
    diagonal_one = (base_one[0] - total(parts_diagonal)).astype(BF16)
    chosen = choose(nodes, parent_two, diagonal_one, exchange(diagonal_one, CORE, 1))
    diagonals = [chosen[0]] + [exchange(chosen[t], CHIP, t) for t in range(1, nodes)]
    parts_last = spread(total(parts_small).astype(BF16), ROW)
    upper, diagonal_two = form_last(parent_two, link_two[0], base_two[0], diagonals, parts_last)
    column_two = form_sum([columns[0], *parts_two])
    return (
        column_one[None],
        diagonal_one[None],
        column_two[None],
        upper[None],
        diagonal_two[None],
    )


def solution(mesh):
    rows, columns = mesh.devices.shape
    fine = Mesh(mesh.devices.reshape(rows, columns // 2, 2), (ROW, CHIP, CORE))
    col = (CHIP, CORE)
    return jax.shard_map(
        local,
        mesh=fine,
        in_specs=(
            P(ROW, col, None, None),
            P(),
            P(col, ROW, None, None),
            P(col, None, None),
            P(),
            P(),
            P(col, ROW, None, None),
            P(col, None, None),
            P(col, None, None),
        ),
        out_specs=(
            P(col, ROW, None, None),
            P(col, None, None),
            P(col, ROW, None, None),
            P(col, None, None),
            P(col, None, None),
        ),
        check_vma=False,
    )
```

```python
import functools

import jax
import jax.numpy as jnp
from jax import lax
from jax.experimental import pallas as pl
from jax.experimental.pallas import tpu as pltpu
from jax.sharding import Mesh, PartitionSpec as P

ROW, CHIP, CORE = "prow", "pchip", "pcore"
F32 = jnp.float32
BF16 = jnp.bfloat16
SMEM = pl.BlockSpec(memory_space=pltpu.SMEM)
VMEM = pl.BlockSpec(memory_space=pltpu.VMEM)
LIMIT = 24 << 20
PARTS = 4


HBM = pl.BlockSpec(memory_space=pltpu.HBM)
ANY = pl.BlockSpec(memory_space=pl.ANY)


def begin(copies):
    for copy in copies:
        copy.start()
    return copies


def finish(copies):
    for copy in copies:
        copy.wait()


def load(own, sibling, inverse, sems):
    core, step = lax.axis_index(CORE), own.shape[0] // PARTS
    copies = []
    for n in range(PARTS):
        rows = pl.ds(n * step, step)
        for k, (ref, at) in enumerate(((own, core), (sibling, 1 - core))):
            copies.append(
                pltpu.make_async_copy(ref.at[rows], inverse.at[at, rows], sems.at[2 * n + k])
            )
    return begin(copies)


def pair_kernel(own, sibling, inverse, sems):
    finish(load(own, sibling, inverse, sems))


def pair(own, sibling):
    return pl.pallas_call(
        pair_kernel,
        out_shape=jax.ShapeDtypeStruct((2,) + own.shape, BF16),
        in_specs=[ANY] * 2,
        out_specs=VMEM,
        scratch_shapes=[pltpu.SemaphoreType.DMA((2 * PARTS,))],
        compiler_params=pltpu.CompilerParams(vmem_limit_bytes=LIMIT),
        name="pair",
    )(own, sibling)


def positions(count, group, here):
    return [(here ^ s) * group + g for s in range(count) for g in range(group)]


def block(inverse, rows, cols):
    width = inverse.shape[2]
    lines = []
    for row in rows:
        tiles = [inverse[col // width, row, col % width] for col in cols]
        lines.append(jnp.concatenate(tiles, axis=1))
    return jnp.concatenate(lines, axis=0)


def level_one_kernel(nodes, count, rows_one, inverse, *refs):
    here, chip, core = lax.axis_index(ROW), lax.axis_index(CHIP), lax.axis_index(CORE)
    pieces, whole = refs[:count], refs[count]
    group, tile = pieces[0].shape[1], pieces[0].shape[2]
    per_row = group * count
    height, width = inverse.shape[1], 2 * inverse.shape[2]
    for at in range(nodes):
        node = 2 * at + core
        rows = [rows_one[node, here * per_row + m] - here * height for m in range(per_row)]
        cols = [
            rows_one[node, chip * per_row + n] - chip * width
            for n in positions(count, group, here)
        ]
        panel = jnp.concatenate([piece[at].reshape(group * tile, tile) for piece in pieces], axis=0)
        part = jnp.dot(block(inverse, rows, cols), panel, preferred_element_type=F32)
        whole[at] = part.astype(BF16).reshape(per_row, tile, tile)


def near_kernel(
    nodes, choices, parent_two, order_two, own, sibling, ours, theirs, *refs
):
    here, chip, core = lax.axis_index(ROW), lax.axis_index(CHIP), lax.axis_index(CORE)
    inputs, (near, smalls, inverse, sems) = refs[: sum(choices)], refs[sum(choices) :]
    per_row, tile = near.shape[1], near.shape[2]
    copies = load(own, sibling, inverse, sems)
    is_end = jnp.logical_or(chip == 0, chip == nodes - 1)
    for t in range(nodes):
        mine, inputs = inputs[: choices[t]], inputs[choices[t] :]
        factor = mine[0][:per_row]
        if len(mine) > 1:
            factor = jnp.where(is_end, mine[1][:per_row], factor)
        node = 2 * (chip ^ t) + core
        parent = parent_two[node]
        is_ours = parent % 2 == core
        for m in range(per_row):
            at = order_two[node, here * per_row + m] - here * per_row
            near[t, m] = jnp.where(is_ours, ours[parent // 2, at], theirs[parent // 2, at])
        smalls[t] = lax.dot_general(
            near[t].reshape(per_row * tile, tile),
            factor.reshape(per_row * tile, tile),
            (((0,), (0,)), ((), ())),
            preferred_element_type=F32,
        ).astype(BF16)
    finish(copies)


def level_two_kernel(
    nodes, count, choices, rows_one, parent_two, order_two, inverse, near, upper, *refs
):
    here, chip, core = lax.axis_index(ROW), lax.axis_index(CHIP), lax.axis_index(CORE)
    pieces, refs = refs[:count], refs[count:]
    inputs, refs = refs[: sum(choices)], refs[sum(choices) :]
    columns, smalls = refs[:nodes], refs[nodes:]
    group, tile = pieces[0].shape[1], pieces[0].shape[2]
    per_row = group * count
    height, width = inverse.shape[1], 2 * inverse.shape[2]
    is_end = jnp.logical_or(chip == 0, chip == nodes - 1)
    factors = []
    for t in range(nodes):
        mine, inputs = inputs[: choices[t]], inputs[choices[t] :]
        factor = mine[0][...]
        if len(mine) > 1:
            factor = jnp.where(is_end, mine[1][...], factor)
        factors.append(factor[:per_row].reshape(per_row * tile, tile))
        node = 2 * (chip ^ t) + core
        parent = parent_two[node]
        rows = [
            rows_one[parent, order_two[node, here * per_row + m]] - here * height
            for m in range(per_row)
        ]
        cols = [
            rows_one[parent, order_two[node, chip * per_row + n]] - chip * width
            for n in positions(count, group, here)
        ]
        panel = [piece[chip ^ t].reshape(group * tile, tile) for piece in pieces]
        panel = jnp.concatenate(panel, axis=0)
        carried = jnp.dot(
            near[t].reshape(per_row * tile, tile), factor[per_row], preferred_element_type=F32
        )
        part = jnp.dot(block(inverse, rows, cols), panel, preferred_element_type=F32)
        columns[t][...] = (part - carried).astype(BF16).reshape(per_row, tile, tile)
        smalls[t][0] = upper[t]
    for t in range(nodes):
        smalls[t][1] = lax.dot_general(
            factors[t],
            columns[t][...].reshape(per_row * tile, tile),
            (((0,), (0,)), ((), ())),
            preferred_element_type=F32,
        ).astype(BF16)


def cut_kernel(panel, *outs):
    here = lax.axis_index(ROW)
    for s, out in enumerate(outs):
        group = out.shape[0]
        out[...] = panel[pl.ds(pl.multiple_of((here ^ s) * group, group), group)]


def cut_groups(panel, count):
    group = (panel.shape[0] // count,) + panel.shape[1:]
    return pl.pallas_call(
        cut_kernel,
        out_shape=[jax.ShapeDtypeStruct(group, BF16)] * count,
        in_specs=[VMEM],
        out_specs=[VMEM] * count,
        compiler_params=pltpu.CompilerParams(vmem_limit_bytes=LIMIT),
        name="cut_groups",
    )(panel)


def join_kernel(*refs):
    here = lax.axis_index(ROW)
    for s, ref in enumerate(refs[:-1]):
        refs[-1][here ^ s] = ref[...]


def join_groups(groups):
    return pl.pallas_call(
        join_kernel,
        out_shape=jax.ShapeDtypeStruct((len(groups),) + groups[0].shape, BF16),
        in_specs=[VMEM] * len(groups),
        out_specs=VMEM,
        compiler_params=pltpu.CompilerParams(vmem_limit_bytes=LIMIT),
        name="join_groups",
    )(*groups)


def column_kernel(parts, panel, column, part):
    column[...] = (-jnp.sum(parts[...].astype(F32), axis=0)).astype(BF16)
    shape = (panel.shape[0] * panel.shape[1], panel.shape[2])
    part[...] = lax.dot_general(
        panel[...].reshape(shape),
        column[...].reshape(shape),
        (((0,), (0,)), ((), ())),
        preferred_element_type=F32,
    ).astype(BF16)


def form_column(parts, panel):
    return pl.pallas_call(
        column_kernel,
        out_shape=[
            jax.ShapeDtypeStruct(panel.shape, BF16),
            jax.ShapeDtypeStruct(panel.shape[1:], BF16),
        ],
        in_specs=[VMEM] * 2,
        out_specs=[VMEM] * 2,
        compiler_params=pltpu.CompilerParams(vmem_limit_bytes=LIMIT),
        name="form_column",
    )(parts, panel)


def sum_kernel(*refs):
    refs[-1][...] = (-total([ref[...] for ref in refs[:-1]])).astype(BF16)


def form_sum(parts):
    return pl.pallas_call(
        sum_kernel,
        out_shape=jax.ShapeDtypeStruct(parts[0].shape, BF16),
        in_specs=[VMEM] * len(parts),
        out_specs=VMEM,
        compiler_params=pltpu.CompilerParams(vmem_limit_bytes=LIMIT),
        name="form_sum",
    )(*parts)


def choose_kernel(nodes, parent_two, ours, theirs, *outs):
    chip, core = lax.axis_index(CHIP), lax.axis_index(CORE)
    for t in range(nodes):
        parent = parent_two[2 * (chip ^ t) + core]
        outs[t][...] = jnp.where(parent % 2 == core, ours[...], theirs[...])


def choose(nodes, parent_two, ours, theirs):
    return pl.pallas_call(
        functools.partial(choose_kernel, nodes),
        out_shape=[jax.ShapeDtypeStruct(ours.shape, BF16)] * nodes,
        in_specs=[SMEM] + [VMEM] * 2,
        out_specs=[VMEM] * nodes,
        compiler_params=pltpu.CompilerParams(vmem_limit_bytes=LIMIT),
        name="choose",
    )(parent_two, ours, theirs)


def last_kernel(nodes, parent_two, link, base, *refs):
    diagonals, parts, (upper, diagonal_two) = refs[:nodes], refs[nodes:-2], refs[-2:]
    chip, core = lax.axis_index(CHIP), lax.axis_index(CORE)
    step = (parent_two[2 * chip + core] // 2) ^ chip
    near = diagonals[0][...]
    for t in range(1, nodes):
        near = jnp.where(step == t, diagonals[t][...], near)
    sums = total([part[...] for part in parts])
    parent_term = jnp.dot(near, link[...], preferred_element_type=F32)
    upper[...] = (sums[0] - parent_term).astype(BF16)
    term = lax.dot_general(
        link[...], upper[...], (((0,), (0,)), ((), ())), preferred_element_type=F32
    )
    diagonal_two[...] = (base[...] - term + sums[1]).astype(BF16)


def form_last(parent_two, link, base, diagonals, parts):
    return pl.pallas_call(
        functools.partial(last_kernel, len(diagonals)),
        out_shape=[jax.ShapeDtypeStruct(link.shape, BF16)] * 2,
        in_specs=[SMEM] + [VMEM] * (2 + len(diagonals) + len(parts)),
        out_specs=[VMEM] * 2,
        compiler_params=pltpu.CompilerParams(vmem_limit_bytes=LIMIT),
        name="form_last",
    )(parent_two, link, base, *diagonals, *parts)


def level_one(rows_one, inverse, pieces):
    nodes, group, tile = pieces[0].shape[0], pieces[0].shape[1], pieces[0].shape[2]
    count = len(pieces)
    per_row = group * count
    flops = 2 * nodes * per_row * per_row * tile**3
    return pl.pallas_call(
        functools.partial(level_one_kernel, nodes, count),
        out_shape=jax.ShapeDtypeStruct((nodes, per_row, tile, tile), BF16),
        in_specs=[SMEM] + [VMEM] * (1 + count),
        out_specs=VMEM,
        compiler_params=pltpu.CompilerParams(vmem_limit_bytes=LIMIT),
        cost_estimate=pl.CostEstimate(flops=flops, bytes_accessed=12 << 20, transcendentals=0),
        name="level_one",
    )(rows_one, inverse, *pieces)


def form_near(parent_two, order_two, own, sibling, ours, theirs, factors):
    nodes, tiles = ours.shape[0], ours.shape[1:]
    choices = [len(f) for f in factors]
    return pl.pallas_call(
        functools.partial(near_kernel, nodes, choices),
        out_shape=[
            jax.ShapeDtypeStruct(ours.shape, BF16),
            jax.ShapeDtypeStruct((nodes,) + tiles[1:], BF16),
            jax.ShapeDtypeStruct((2,) + own.shape, BF16),
        ],
        in_specs=[SMEM] * 2 + [ANY] * 2 + [VMEM] * (2 + sum(choices)),
        out_specs=[VMEM] * 3,
        scratch_shapes=[pltpu.SemaphoreType.DMA((2 * PARTS,))],
        compiler_params=pltpu.CompilerParams(vmem_limit_bytes=LIMIT),
        name="form_near",
    )(parent_two, order_two, own, sibling, ours, theirs, *sum(factors, []))


def level_two(rows_one, parent_two, order_two, inverse, near, upper, pieces, factors):
    nodes, group, tile = pieces[0].shape[0], pieces[0].shape[1], pieces[0].shape[2]
    count = len(pieces)
    per_row = group * count
    flops = 2 * nodes * per_row * (per_row + 3) * tile**3
    choices = [len(f) for f in factors]
    return pl.pallas_call(
        functools.partial(level_two_kernel, nodes, count, choices),
        out_shape=[jax.ShapeDtypeStruct((per_row, tile, tile), BF16)] * nodes
        + [jax.ShapeDtypeStruct((2, tile, tile), BF16)] * nodes,
        in_specs=[SMEM] * 3 + [VMEM] * (3 + count + sum(choices)),
        out_specs=[VMEM] * (2 * nodes),
        compiler_params=pltpu.CompilerParams(vmem_limit_bytes=LIMIT),
        cost_estimate=pl.CostEstimate(flops=flops, bytes_accessed=16 << 20, transcendentals=0),
        name="level_two",
    )(rows_one, parent_two, order_two, inverse, near, upper, *pieces, *sum(factors, []))


def exchange(x, axis, step):
    size = lax.axis_size(axis)
    return lax.ppermute(x, axis, [(i, i ^ step) for i in range(size)])


def spread(x, axis):
    return [x] + [exchange(x, axis, s) for s in range(1, lax.axis_size(axis))]


def after(x, *others):
    return lax.optimization_barrier((x,) + others)[0]


def together(*arrays):
    return lax.optimization_barrier(arrays)


def halves(panel, axis):
    rows = lax.axis_size(axis)
    return panel.reshape((rows, panel.shape[0] // rows) + panel.shape[1:])


def swap(blocks, axis):
    return lax.all_to_all(blocks, axis, 0, 0, tiled=True)


def total(parts):
    return functools.reduce(jnp.add, [part.astype(F32) for part in parts])


def local(
    inverse_top, rows_one, panel_one, base_one, parent_two, order_two, panel_two, link_two, base_two
):
    chip, core = lax.axis_index(CHIP), lax.axis_index(CORE)
    nodes = lax.axis_size(CHIP)
    line = nodes == 4
    payload = jnp.concatenate([panel_two[0], link_two], axis=0)
    near = exchange(payload, CHIP, 1)
    if line:
        inner = lax.ppermute(payload, CHIP, [(1, 2), (2, 1)])
    else:
        inner = [exchange(payload, CHIP, t) for t in range(2, nodes)]
    sibling = exchange(inverse_top, CORE, 1)
    quarters = swap(halves(panel_one[0], ROW), ROW)
    kept, *sends = cut_groups(panel_two[0], lax.axis_size(ROW))
    quarters, near, inner, sends = together(quarters, near, inner, sends)
    blocks_one = swap(quarters, CHIP)
    groups = [kept] + [exchange(send, ROW, s + 1) for s, send in enumerate(sends)]
    quarters_two = join_groups(groups)
    pieces_one = spread(blocks_one, ROW)
    inverse = pair(inverse_top, after(sibling, blocks_one))
    quarters_two, payload_late, near_late, inner_late = together(
        quarters_two, payload, near, inner, blocks_one
    )[:4]
    blocks_two = swap(quarters_two, CHIP)
    over = out_one = ()
    if line:
        is_end = jnp.logical_or(chip == 0, chip == nodes - 1)
        over = exchange(jnp.where(is_end, payload_late, near_late), CHIP, nodes - 1)
        out_one = lax.ppermute(inner_late, CHIP, [(1, 0), (2, 3)])
    ours = level_one(rows_one, inverse, pieces_one)
    ours, blocks_two, over, out_one = together(ours, blocks_two, over, out_one)
    theirs = exchange(ours, CORE, 1)
    parts_one = swap(ours, CHIP)
    pieces_two = spread(blocks_two, ROW)
    if line:
        factors = [[payload], [near], [over, out_one], [inner, over]]
    else:
        factors = [[f] for f in [payload, near, *inner]]
    near_two, upper_part, inverse = form_near(
        parent_two, order_two, inverse_top, sibling, ours, theirs, factors
    )
    outs = level_two(
        rows_one, parent_two, order_two, inverse, near_two, upper_part, pieces_two, factors
    )
    columns, smalls = outs[:nodes], outs[nodes:]
    parts_small = [smalls[0]] + [exchange(smalls[t], CHIP, t) for t in range(1, nodes)]
    first = [exchange(columns[2], CHIP, 2)]
    column_one, part = form_column(parts_one, panel_one[0])
    columns, parts_small, parts_diagonal = together(columns, parts_small, spread(part, ROW))
    parts_two = [exchange(columns[t], CHIP, t) for t in range(1, nodes) if t != 2] + first
    diagonal_one = (base_one[0] - total(parts_diagonal)).astype(BF16)
    chosen = choose(nodes, parent_two, diagonal_one, exchange(diagonal_one, CORE, 1))
    diagonals = [chosen[0]] + [exchange(chosen[t], CHIP, t) for t in range(1, nodes)]
    parts_last = spread(total(parts_small).astype(BF16), ROW)
    upper, diagonal_two = form_last(parent_two, link_two[0], base_two[0], diagonals, parts_last)
    column_two = form_sum([columns[0], *parts_two])
    return (
        column_one[None],
        diagonal_one[None],
        column_two[None],
        upper[None],
        diagonal_two[None],
    )


def solution(mesh):
    rows, columns = mesh.devices.shape
    fine = Mesh(mesh.devices.reshape(rows, columns // 2, 2), (ROW, CHIP, CORE))
    col = (CHIP, CORE)
    return jax.shard_map(
        local,
        mesh=fine,
        in_specs=(
            P(ROW, col, None, None),
            P(),
            P(col, ROW, None, None),
            P(col, None, None),
            P(),
            P(),
            P(col, ROW, None, None),
            P(col, None, None),
            P(col, None, None),
        ),
        out_specs=(
            P(col, ROW, None, None),
            P(col, None, None),
            P(col, ROW, None, None),
            P(col, None, None),
            P(col, None, None),
        ),
        check_vma=False,
    )
```
